512 devices in a mesh: cp: 32 (over z, x_hi), tp: 4 (over x_lo, core), dp: 4 (over y).
Axes of the slice: x: 4 (x_hi: 2, x_lo: 2; x = x_hi * 2 + x_lo), y: 4, z: 16, core: 2. Of those that a mesh axis runs over, the one named last changes fastest.
Arguments:
- q_proj: bfloat16 [4096, 4096], P('cp', ('tp', 'dp')), may hold values from -18 to 18
- key_projection: bfloat16 [4096, 256], P('cp'), may hold values from -18 to 18
- value_projection: bfloat16 [4096, 256], P('cp'), may hold values from -6 to 6
- segments: int32 [4096], replicated, may hold values from 0 to 7, never falling along the last dimension, each value on 1 to 2048 neighbouring positions
- resid: bfloat16 [4096, 4096], P('cp', ('tp', 'dp')), may hold values from -6 to 6
- norm_gain: bfloat16 [4096], replicated, may hold values from 0.5 to 1.5
- route_ids: int32 [4096, 8], P(('cp', 'dp')), may hold values from 0 to 127, all different within a row; in each aligned block of 32 rows (0 to 31, 32 to 63, ...) at most 4 rows name the same one
- route_gates: float32 [4096, 8], P(('cp', 'dp')), may hold values from 0.05 to 0.5
- w_gate: bfloat16 [128, 768, 4096], P(('cp', 'dp'), 'tp'), may hold values from -0.09375 to 0.09375
- w_up: bfloat16 [128, 768, 4096], P(('cp', 'dp'), 'tp'), may hold values from -0.09375 to 0.09375
- w_down: bfloat16 [128, 768, 4096], P(('cp', 'dp'), None, 'tp'), may hold values from -0.21875 to 0.21875
Outputs:
- mixed: bfloat16 [4096, 4096], P(('cp', 'dp'), 'tp')
The draws below stay inside these ranges and needn't reach their ends.
Inputs may be any that keep to these rules, and one draw needn't show every extreme that they name: `route_ids`: each row names 8 different experts; in each aligned block of 32 rows no expert is named by more than 4 rows, and in every block some expert is named by exactly 4. `segments`: document numbers never fall along the sequence; a document spans 1 to 2048 positions, one exactly that many.
All inputs are finite; a program needn't handle non-finite values.
Results may differ from the reference program's by a relative error of at most 0.006.
Values may be sent and summed in bfloat16 or wider, within the bound.
A program may use at most 64 MiB of HBM per device.

```python
import math
import jax
import jax.numpy as jnp
import numpy as np
from jax import lax

D = 4096
QUERY_HEADS = 32
KEY_VALUE_HEADS = 2
HEAD_WIDTH = 128
HID = 768
TOPK = 8
DOCS = 8
SEQUENCE_LENGTH = 4096
ROWS_DEV = 32
EXPERTS = 128
CAP = 4


def draw_key_projection(key, part):
    key = jax.random.fold_in(key, 1)
    layer_output = jnp.clip(jax.random.normal(key, (SEQUENCE_LENGTH, KEY_VALUE_HEADS * HEAD_WIDTH), jnp.float32), -4.0, 4.0)
    return layer_output.astype(jnp.bfloat16)


def draw_q_proj(key, part):
    key = jax.random.fold_in(key, 2)
    layer_output = jnp.clip(jax.random.normal(key, (SEQUENCE_LENGTH, QUERY_HEADS * HEAD_WIDTH), jnp.float32), -4.0, 4.0)
    return layer_output.astype(jnp.bfloat16)


def block_levels(own_key, extent, split, least, high):
    loudness, own = 1.0, jax.random.fold_in(own_key, 6)
    for position, blocks in split:
        draws = jnp.exp(jax.random.uniform(jax.random.fold_in(own, position), (blocks,), jnp.float32, least / len(split), high / len(split)))
        loudness = loudness * jnp.repeat(draws, extent[position] // blocks).reshape([-1 if axis == position else 1 for axis in range(len(extent))])
    return loudness


def profile(count, total, reach, skew):
    weights = [(1 << 20) // math.isqrt(standing ** skew) + 1 for standing in range(2, count + 1)]
    surplus, counts = total - reach - (count - 1), [1] * (count - 1)
    while surplus > 0:
        candidates = [i for i in range(count - 1) if counts[i] < reach]
        whole, left = sum([weights[i] for i in candidates]), surplus
        for i in candidates:
            extra = min(reach - counts[i], max(1, left * weights[i] // whole), surplus)
            counts[i] = counts[i] + extra
            surplus = surplus - extra
    return np.array([reach] + counts)


def ragged(own_key, count, total, reach, lean):
    if count == 2:
        one = jax.random.randint(own_key, (), max(1, total - reach), min(reach, total - 1) + 1)
        return jnp.stack([one, total - one])
    lengths = jnp.asarray(profile(count, total, reach, lean), jnp.int32)
    pairs = (count - 1) // 2
    donor, sink = lengths[1:1 + 2 * pairs:2], lengths[2:2 + 2 * pairs:2]
    room = jnp.minimum(donor - 1, reach - sink)
    moved = jax.random.randint(jax.random.fold_in(own_key, 1), (pairs,), 0, 1 << 20) % (room + 1)
    lengths = lengths.at[1:1 + 2 * pairs:2].set(donor - moved).at[2:2 + 2 * pairs:2].set(sink + moved)
    return lengths[jax.random.permutation(jax.random.fold_in(own_key, 2), count)]


def shared_out(stream_key, own, number, rows, count, top, bound, slope):
    order = jax.random.permutation(stream_key, count)
    crowded, common = portions_of(count, rows * top, bound, slope, True), portions_of(count, rows * top, bound, slope, False)
    places = jnp.arange(count)

    def named(sizes, rotation):
        used = int((sizes > 0).sum())
        fixed = max(1, used // 4)
        passed = fixed + (places - fixed + rotation * (used - fixed)) % max(1, count - fixed)
        return jnp.zeros((count,), jnp.int32).at[order[jnp.where(places < fixed, places, passed)]].set(jnp.asarray(sizes, jnp.int32))

    sizes = jnp.where(number % 4 == 0, named(crowded, number // 4), named(common, number - number // 4 - 1))
    mixed = jax.random.permutation(jax.random.fold_in(own, 3), count)
    donor, receiver = mixed[0:count // 2 * 2:2], mixed[1:count // 2 * 2:2]
    room = jnp.minimum(sizes[donor] - 1, bound - sizes[receiver]) // 2
    room = jnp.where((donor == order[0]) | (receiver == order[0]) | (sizes[receiver] == 0), 0, jnp.maximum(room, 0))
    passed = jax.random.randint(jax.random.fold_in(own, 4), (count // 2,), 0, 1 << 20) % (room + 1)
    sizes = sizes.at[donor].add(-passed).at[receiver].add(passed)
    items = jnp.searchsorted(jnp.cumsum(sizes), jnp.arange(rows * top), side="right").astype(jnp.int32)
    grid = items.reshape(top, rows).T
    grid = grid[jax.random.permutation(jax.random.fold_in(own, 1), rows)]
    rotation = jax.random.randint(jax.random.fold_in(own, 2), (rows, 1), 0, top)
    return jnp.take_along_axis(grid, (jnp.arange(top)[None, :] + rotation) % top, axis=1)


def portions_of(count, total, reach, skew, full):
    portions = [(1 << 20) // math.isqrt(standing ** skew) + 1 for standing in range(1, count + 1)]
    largest = reach if full else min(reach, max(-(-total // count), total * portions[0] // sum(portions)))
    least = 1 if total - largest >= count - 1 else 0
    holding, rest = [largest] + [least] * (count - 1), total - largest - least * (count - 1)
    while rest > 0:
        candidates = [i for i in range(1, count) if holding[i] < largest] or [i for i in range(1, count) if holding[i] < reach]
        pool, left = sum([portions[i] for i in candidates]), rest
        for i in candidates:
            more = min(reach - holding[i], max(1, left * portions[i] // pool), rest)
            holding[i] = holding[i] + more
            rest = rest - more
    return np.array(holding)


def scatter_about(key, extent, scale, limit, cuts=(), kind=jnp.bfloat16):
    values = scale * jax.random.normal(key, extent, jnp.float32)
    if cuts:
        values = values * block_levels(key, extent, cuts, -0.22, 0.18)
    return jnp.clip(values, -limit, limit).astype(kind)


def setup_inputs(seed: int = 0) -> dict:
    splits = jax.random.split(jax.random.key(seed), 12)
    q_proj = draw_q_proj(jax.random.fold_in(splits[11], 71), 0)
    key_projection = draw_key_projection(jax.random.fold_in(splits[11], 71), 0)
    value_projection = scatter_about(splits[2], (SEQUENCE_LENGTH, KEY_VALUE_HEADS * HEAD_WIDTH), 1.0, 6.0, ((0, 32),))
    segments = jnp.searchsorted(jnp.cumsum(ragged(splits[3], DOCS, SEQUENCE_LENGTH, SEQUENCE_LENGTH // 2, 0)), jnp.arange(SEQUENCE_LENGTH), side="right").astype(jnp.int32)
    resid = scatter_about(splits[4], (SEQUENCE_LENGTH, D), 1.0, 6.0, ((0, 32), (1, 16)))
    norm_gain = jnp.clip(1.0 + 0.1 * jax.random.normal(splits[5], (D,), jnp.float32), 0.5, 1.5).astype(jnp.bfloat16)
    route_ids_keys = jax.random.split(jax.random.fold_in(splits[6], 1), SEQUENCE_LENGTH // ROWS_DEV)
    route_ids_turns = jax.random.permutation(jax.random.fold_in(splits[6], 3), SEQUENCE_LENGTH // ROWS_DEV)
    route_ids = jax.vmap(lambda own, number: shared_out(jax.random.fold_in(splits[6], 2), own, number, ROWS_DEV, EXPERTS, TOPK, CAP, 2))(route_ids_keys, route_ids_turns).reshape((SEQUENCE_LENGTH, TOPK))
    route_gates = jnp.clip(jnp.exp(math.log(0.5) - 2.3025851 * jax.random.uniform(splits[7], (SEQUENCE_LENGTH, TOPK), jnp.float32) ** block_levels(splits[7], (SEQUENCE_LENGTH, TOPK), ((0, 128),), -0.2, 0.2)), 0.05, 0.5)
    w_gate = scatter_about(splits[8], (EXPERTS, HID, D), D ** -0.5, 0.09375, ((0, 128), (1, 4)))
    w_up = scatter_about(splits[9], (EXPERTS, HID, D), D ** -0.5, 0.09375, ((0, 128), (1, 4)))
    w_down = scatter_about(splits[10], (EXPERTS, HID, D), HID ** -0.5, 0.21875, ((0, 128), (2, 4)))
    return dict(q_proj=q_proj, key_projection=key_projection, value_projection=value_projection, segments=segments, resid=resid, norm_gain=norm_gain, route_ids=route_ids, route_gates=route_gates, w_gate=w_gate, w_up=w_up, w_down=w_down)


epsilon = 1e-06
masked_score = -1e+30

def expert_apply(tokens_in, gate_rows, up_rows, down_rows):
    contract = (((1,), (1,)), ((), ()))
    gate_val = lax.dot_general(tokens_in, gate_rows, contract, preferred_element_type=jnp.float32)
    up_val = lax.dot_general(tokens_in, up_rows, contract, preferred_element_type=jnp.float32)
    hidden = (jax.nn.silu(gate_val) * up_val).astype(jnp.bfloat16)
    return jnp.dot(hidden, down_rows, preferred_element_type=jnp.float32).astype(jnp.bfloat16)

def reference(q_proj, key_projection, value_projection, segments, resid, norm_gain, route_ids, route_gates, w_gate, w_up, w_down):
    group_width = QUERY_HEADS // KEY_VALUE_HEADS
    score_scale = HEAD_WIDTH ** (-0.5)
    positions = jnp.arange(SEQUENCE_LENGTH, dtype=jnp.int32)
    allowed = (positions[None, :] <= positions[:, None]) & (segments[None, :] == segments[:, None])
    q_all = q_proj.reshape(SEQUENCE_LENGTH, QUERY_HEADS, HEAD_WIDTH)
    key_rows_total = key_projection.reshape(SEQUENCE_LENGTH, KEY_VALUE_HEADS, HEAD_WIDTH)
    value_rows_total = value_projection.reshape(SEQUENCE_LENGTH, KEY_VALUE_HEADS, HEAD_WIDTH)

    def head_output(head_index):
        query_rows = q_all[:, head_index]
        keys_here = key_rows_total[:, head_index // group_width]
        values_here = value_rows_total[:, head_index // group_width]
        scores = jnp.dot(query_rows, keys_here.T, preferred_element_type=jnp.float32) * score_scale
        scores = jnp.where(allowed, scores, masked_score)
        weights = jnp.exp(scores - lax.optimization_barrier(jnp.max(scores, 1, keepdims=True)))
        row_total = lax.optimization_barrier(jnp.sum(weights, 1, keepdims=True))
        return jnp.dot(weights.astype(jnp.bfloat16), values_here, preferred_element_type=jnp.float32) / row_total
    heads_out = lax.map(head_output, jnp.arange(QUERY_HEADS, dtype=jnp.int32))
    attended = heads_out.transpose(1, 0, 2).reshape(SEQUENCE_LENGTH, QUERY_HEADS * HEAD_WIDTH)
    after_attn = (resid.astype(jnp.float32) + attended).astype(jnp.bfloat16)
    values = after_attn.astype(jnp.float32)
    inverse = lax.rsqrt(lax.optimization_barrier(jnp.mean(values * values, 1, keepdims=True)) + epsilon)
    normed = (values * inverse * norm_gain.astype(jnp.float32)).astype(jnp.bfloat16)
    expert_slots = SEQUENCE_LENGTH // ROWS_DEV * CAP
    flat_ids = route_ids.reshape(-1).astype(jnp.int32)
    one_hot = (flat_ids[:, None] == jnp.arange(EXPERTS, dtype=jnp.int32)[None, :]).astype(jnp.int32)
    slot_number = lax.optimization_barrier(jnp.sum((jnp.cumsum(one_hot, 0) - one_hot) * one_hot, 1)).astype(jnp.int32)
    targets = flat_ids * expert_slots + slot_number
    spread = jnp.repeat(normed, TOPK, 0)
    slot_table = jnp.zeros((EXPERTS * expert_slots, D), jnp.bfloat16).at[targets].set(spread)
    slot_table = slot_table.reshape(EXPERTS, expert_slots, D)
    produced = lax.map(lambda expert: expert_apply(slot_table[expert], w_gate[expert], w_up[expert], w_down[expert]), jnp.arange(EXPERTS, dtype=jnp.int32))
    picked = produced.reshape(EXPERTS * expert_slots, D)[targets].reshape(SEQUENCE_LENGTH, TOPK, D)
    expert_sum = jnp.einsum('rj,rjd->rd', route_gates, picked.astype(jnp.float32))
    return (after_attn.astype(jnp.float32) + expert_sum).astype(jnp.bfloat16)
```

```python
import jax
import jax.numpy as jnp
from jax import lax
from jax.sharding import Mesh, PartitionSpec as P

QUERY_HEADS = 32
KEY_VALUE_HEADS = 2
HEAD_WIDTH = 128
CAP = 4
WINDOW = 17

epsilon = 1e-06
masked_score = -1e30


def attend(q_proj, key_projection, value_projection, segments):
    rows = q_proj.shape[0]
    heads = q_proj.shape[1] // HEAD_WIDTH
    context = lax.axis_index("z") * lax.axis_size("xh") + lax.axis_index("xh")
    blocks = lax.axis_size("z") * lax.axis_size("xh")
    kv_head = lax.axis_index("xl")
    k_mine = lax.dynamic_slice_in_dim(key_projection, kv_head * HEAD_WIDTH, HEAD_WIDTH, 1)
    v_mine = lax.dynamic_slice_in_dim(value_projection, kv_head * HEAD_WIDTH, HEAD_WIDTH, 1)
    kv = lax.all_gather(jnp.concatenate([k_mine, v_mine], 1), ("z", "xh"), axis=0, tiled=True)
    window = min(WINDOW, blocks) * rows
    first_key = jnp.maximum(context + 1 - WINDOW, 0) * rows
    kv = lax.dynamic_slice_in_dim(kv, first_key, window, 0)
    k_all, v_all = kv[:, :HEAD_WIDTH], kv[:, HEAD_WIDTH:]
    seg_keys = lax.dynamic_slice_in_dim(segments, first_key, window, 0)
    first_row = context * rows
    seg_rows = lax.dynamic_slice_in_dim(segments, first_row, rows, 0)
    q_positions = first_row + jnp.arange(rows, dtype=jnp.int32)
    k_positions = first_key + jnp.arange(window, dtype=jnp.int32)
    allowed = (k_positions[None, :] <= q_positions[:, None]) & (
        seg_keys[None, :] == seg_rows[:, None]
    )
    q_heads = q_proj.reshape(rows, heads, HEAD_WIDTH)
    scores = jnp.einsum("rhd,kd->hrk", q_heads, k_all, preferred_element_type=jnp.float32)
    scores = jnp.where(allowed[None], scores * HEAD_WIDTH ** (-0.5), masked_score)
    weights = jnp.exp(scores - jnp.max(scores, 2, keepdims=True))
    total = jnp.sum(weights, 2)
    mixed = jnp.einsum(
        "hrk,kd->hrd", weights.astype(jnp.bfloat16), v_all, preferred_element_type=jnp.float32
    )
    return (mixed / total[:, :, None]).transpose(1, 0, 2).reshape(rows, heads * HEAD_WIDTH)


def body(
    q_proj,
    key_projection,
    value_projection,
    segments,
    resid,
    norm_gain,
    route_ids,
    route_gates,
    w_gate,
    w_up,
    w_down,
):
    n_z, n_xh, n_dp = lax.axis_size("z"), lax.axis_size("xh"), lax.axis_size("dp")
    n_tensor = lax.axis_size("xl") * lax.axis_size("core")
    tensor_index = lax.axis_index("xl") * lax.axis_size("core") + lax.axis_index("core")
    attended = attend(q_proj, key_projection, value_projection, segments)
    after_attn = (resid.astype(jnp.float32) + attended).astype(jnp.bfloat16)
    folded = lax.all_to_all(after_attn, "dp", split_axis=0, concat_axis=1, tiled=True)
    rows, width = folded.shape
    values = folded.astype(jnp.float32)
    squares = lax.psum(jnp.sum(values * values, 1), ("xl", "core"))
    inverse = lax.rsqrt(squares / (width * n_tensor) + epsilon)[:, None]
    gain_here = lax.dynamic_slice_in_dim(norm_gain, tensor_index * width, width, 0)
    normed = (values * inverse * gain_here.astype(jnp.float32)).astype(jnp.bfloat16)

    plane = n_xh * n_dp
    ids = lax.all_gather(route_ids, "z", axis=0)
    gates = lax.all_gather(route_gates, "z", axis=0)
    first_expert = lax.axis_index("z") * plane
    local = first_expert + jnp.arange(plane, dtype=jnp.int32)
    member = ids[:, None, :, :] == local[None, :, None, None]
    named = jnp.any(member, 3)
    weight = jnp.sum(jnp.where(member, gates[:, None], 0.0), 3)
    rank = jnp.cumsum(named.astype(jnp.int32), 2) - 1
    slots = jnp.arange(CAP, dtype=jnp.int32)
    chosen = named[:, :, None, :] & (rank[:, :, None, :] == slots[None, None, :, None])
    picker = chosen.astype(jnp.bfloat16).reshape(n_z, plane * CAP, rows)
    mixer = jnp.where(chosen, weight[:, :, None, :], 0.0).reshape(n_z, plane * CAP, rows)

    tokens = lax.all_gather(normed, "z", axis=0)
    outgoing = jnp.einsum("zsr,zrd->zsd", picker, tokens, preferred_element_type=jnp.float32)
    outgoing = outgoing.astype(jnp.bfloat16).reshape(n_z, plane, CAP, width)
    outgoing = outgoing.transpose(1, 0, 2, 3).reshape(plane, n_z * CAP, width)
    arrived = lax.all_to_all(outgoing, ("xh", "dp"), split_axis=0, concat_axis=0, tiled=True)
    arrived = arrived.reshape(plane * n_z * CAP, width)
    full = lax.all_gather(arrived, ("xl", "core"), axis=1, tiled=True)
    contract = (((1,), (1,)), ((), ()))
    gate_val = lax.dot_general(full, w_gate[0], contract, preferred_element_type=jnp.float32)
    up_val = lax.dot_general(full, w_up[0], contract, preferred_element_type=jnp.float32)
    hidden = (jax.nn.silu(gate_val) * up_val).astype(jnp.bfloat16)
    hidden = lax.all_gather(hidden, ("xl", "core"), axis=1, tiled=True)
    produced = jnp.dot(hidden, w_down[0], preferred_element_type=jnp.float32).astype(jnp.bfloat16)
    returned = lax.all_to_all(
        produced.reshape(plane, n_z * CAP, width), ("xh", "dp"), split_axis=0, concat_axis=0, tiled=True
    )
    returned = returned.reshape(plane, n_z, CAP, width).transpose(1, 0, 2, 3)
    returned = returned.reshape(n_z, plane * CAP, width)
    partial = jnp.einsum(
        "zsr,zsd->zrd",
        mixer,
        returned.astype(jnp.float32),
        precision=lax.Precision.HIGHEST,
        preferred_element_type=jnp.float32,
    )
    expert_sum = lax.psum_scatter(partial, "z", scatter_dimension=0, tiled=False)
    return (values + expert_sum).astype(jnp.bfloat16)


def solution(mesh):
    n_cp, n_tp, n_dp = (mesh.shape[a] for a in ("cp", "tp", "dp"))
    fine = Mesh(
        mesh.devices.reshape(n_cp // 2, 2, n_tp // 2, 2, n_dp), ("z", "xh", "xl", "core", "dp")
    )
    cp, tp = ("z", "xh"), ("xl", "core")
    placed = (
        P(cp, tp + ("dp",)),
        P(cp, None),
        P(cp, None),
        P(),
        P(cp, tp + ("dp",)),
        P(),
        P(cp + ("dp",), None),
        P(cp + ("dp",), None),
        P(cp + ("dp",), tp, None),
        P(cp + ("dp",), tp, None),
        P(cp + ("dp",), None, tp),
    )
    return jax.shard_map(
        body, mesh=fine, in_specs=placed, out_specs=P(cp + ("dp",), tp), check_vma=False
    )
```

```python
import functools

import jax
import jax.numpy as jnp
from jax import lax
from jax.experimental import pallas as pl
from jax.experimental.pallas import tpu as pltpu
from jax.sharding import Mesh, PartitionSpec as P

HEAD_WIDTH = 128
CAP = 4
REACH = 2048
BLOCK = 32
GROUP = 4
SLOTS = GROUP * CAP
SPLIT = 2

epsilon = 1e-06
masked_score = -1e30
bf16, f32 = jnp.bfloat16, jnp.float32
MESH = pl.DeviceIdType.MESH


def sizes():
    return {a: lax.axis_size(a) for a in ("z", "xh", "xl", "core", "dp")}


def places():
    return {a: lax.axis_index(a) for a in ("z", "xh", "xl", "core", "dp")}


def moved(me, n, **steps):
    return {a: lax.rem(me[a] + n[a] + s, n[a]) for a, s in steps.items()}


def shifts(n, axes):
    found = [{}]
    for a in axes:
        found = [{**f, a: s} for f in found for s in range(n[a])]
    return found[1:]


def copy_to(src, dst, send, recv, device):
    return pltpu.make_async_remote_copy(
        src_ref=src, dst_ref=dst, send_sem=send, recv_sem=recv, device_id=device, device_id_type=MESH
    )


def greet(me, n, steps):
    barrier = pltpu.get_barrier_semaphore()
    for s in steps:
        pl.semaphore_signal(barrier, inc=1, device_id=moved(me, n, **s), device_id_type=MESH)
    pl.semaphore_wait(barrier, len(steps))


def up_place(k):
    return 2 * k - 1 if k else 0


def attention_kernel(
    n, q_ref, k_ref, v_ref, seg_ref, resid_ref, gain_ref, ids_ref, gates_ref,
    normed_ref, kept_ref, routes_ref,
    kv, queries, table, routes, stage, fold,
    z_send, z_recv, plane_send, plane_recv, core_send, core_recv,
    route_send, route_recv, fold_send, fold_recv,
):
    me = places()
    rows = q_ref.shape[0]
    heads = q_ref.shape[1] // HEAD_WIDTH
    plane_rows = n["xh"] * rows
    reach = min(-(-REACH // plane_rows), n["z"] - 1)
    up, down = n["z"] // 2, n["z"] // 2 - 1
    plane = shifts(n, ("xh", "dp"))
    group = shifts(n, ("xl", "core", "dp"))
    line = [{"z": s} for s in range(1, n["z"])]
    greet(me, n, line + plane + [g for g in group if g.get("xl") or g.get("core")])

    core = me["core"]
    quarter = rows // n["dp"]
    start = pl.multiple_of(me["xh"] * rows + me["dp"] * quarter, quarter)
    here = pl.ds(start, quarter)
    head = pl.ds(pl.multiple_of(me["xl"] * HEAD_WIDTH, HEAD_WIDTH), HEAD_WIDTH)
    mine = pl.ds(pl.multiple_of(me["dp"] * quarter, quarter), quarter)
    kv[core, 0, here, :] = jnp.where(core == 0, k_ref[mine, head], v_ref[mine, head])
    z_copies = {
        d: copy_to(
            kv.at[core, 0, here], kv.at[core, d, here], z_send.at[d], z_recv.at[d], moved(me, n, z=d)
        )
        for d in range(1, reach + 1)
    }
    for c in z_copies.values():
        c.start()

    def plane_copy(d, i):
        return copy_to(
            kv.at[core, d, here], kv.at[core, d, here],
            plane_send.at[d, i], plane_recv.at[d, i], moved(me, n, **plane[i]),
        )

    def core_copy(d):
        return copy_to(
            kv.at[core, d], kv.at[core, d], core_send.at[d], core_recv.at[d], moved(me, n, core=1)
        )

    for i in range(len(plane)):
        plane_copy(0, i).start()

    lanes = ids_ref.shape[1]
    experts = table.shape[1]
    per_plane = experts // n["z"]
    expert = lax.broadcasted_iota(jnp.int32, (experts, lanes), 0)
    named = jnp.zeros((experts, lanes), f32)
    weight = jnp.zeros((experts, lanes), f32)
    for j in range(ids_ref.shape[0]):
        equal = expert == ids_ref[j : j + 1, :]
        named += jnp.where(equal, 1.0, 0.0)
        weight += jnp.where(equal, gates_ref[j : j + 1, :], 0.0)
    earlier = lax.broadcasted_iota(jnp.int32, (lanes, lanes), 0)
    later = lax.broadcasted_iota(jnp.int32, (lanes, lanes), 1)
    before = (earlier < later) & (earlier // BLOCK == later // BLOCK)
    rank = jnp.dot(
        named.astype(bf16), jnp.where(before, 1.0, 0.0).astype(bf16), preferred_element_type=f32
    )
    table[0] = jnp.where(named > 0.5, rank, 2.0 * CAP)
    table[1] = weight

    def rows_of(plane_index):
        return pl.ds(pl.multiple_of(plane_index * per_plane, per_plane), per_plane)

    route_copies = []
    for k, place in [(k, 2 * k - 1) for k in range(1, up + 1)] + [(-k, 2 * k) for k in range(1, down + 1)]:
        target = moved(me, n, z=k)
        route_copies.append(
            copy_to(
                table.at[:, rows_of(target["z"])], routes.at[place],
                route_send.at[place], route_recv.at[place], target,
            )
        )
        route_copies[-1].start()
    routes[0] = table[:, rows_of(me["z"]), :]

    for h in range(heads):
        queries[h * rows : (h + 1) * rows] = q_ref[:, h * HEAD_WIDTH : (h + 1) * HEAD_WIDTH]
    all_rows = heads * rows
    context = me["z"] * n["xh"] + me["xh"]
    first_row = pl.multiple_of(context * rows, rows)
    seg_here = seg_ref[:, pl.ds(first_row, rows)].astype(f32)
    r = lax.broadcasted_iota(jnp.int32, (all_rows, rows), 0)
    c = lax.broadcasted_iota(jnp.int32, (all_rows, rows), 1)
    seg_rows = jnp.sum(jnp.where(lax.rem(r, rows) == c, seg_here, 0.0), 1, keepdims=True)
    q_position = first_row + lax.rem(
        lax.broadcasted_iota(jnp.int32, (all_rows, plane_rows), 0), rows
    )
    k_offset = lax.broadcasted_iota(jnp.int32, (all_rows, plane_rows), 1)
    state = None
    for t in range(reach + 3):
        if 1 <= t <= reach:
            z_copies[t].wait_recv()
            for i in range(len(plane)):
                plane_copy(t, i).start()
        if 0 <= t - 1 <= reach:
            for i in range(len(plane)):
                plane_copy(t - 1, i).wait_recv()
            core_copy(t - 1).start()
        d = t - 2
        if d < 0:
            continue
        core_copy_back = copy_to(
            kv.at[1 - core, d], kv.at[1 - core, d], core_send.at[d], core_recv.at[d], moved(me, n, core=1)
        )
        core_copy_back.wait_recv()
        first_key = pl.multiple_of(lax.rem(me["z"] + n["z"] - d, n["z"]) * plane_rows, plane_rows)
        scores = (
            lax.dot_general(
                queries[...], kv[0, d], (((1,), (1,)), ((), ())), preferred_element_type=f32
            )
            * HEAD_WIDTH ** (-0.5)
        )
        seg_keys = seg_ref[:, pl.ds(first_key, plane_rows)].astype(f32)
        allowed = (first_key + k_offset <= q_position) & (seg_keys == seg_rows)
        scores = jnp.where(allowed, scores, masked_score)
        top = jnp.max(scores, 1, keepdims=True)
        if state is None:
            weights = jnp.exp(scores - top)
            total = jnp.sum(weights, 1, keepdims=True)
            acc = jnp.dot(weights.astype(bf16), kv[1, d], preferred_element_type=f32)
        else:
            old_top, old_total, old_acc = state
            top = jnp.maximum(old_top, top)
            weights = jnp.exp(scores - top)
            fade = jnp.exp(old_top - top)
            total = old_total * fade + jnp.sum(weights, 1, keepdims=True)
            acc = old_acc * fade + jnp.dot(
                weights.astype(bf16), kv[1, d], preferred_element_type=f32
            )
        state = (top, total, acc)
    attended = state[2] / state[1]
    for h in range(heads):
        cols = slice(h * HEAD_WIDTH, (h + 1) * HEAD_WIDTH)
        stage[:, cols] = (
            resid_ref[:, cols].astype(f32) + attended[h * rows : (h + 1) * rows]
        ).astype(bf16)

    tensor = me["xl"] * n["core"] + core
    slab = tensor * n["dp"] + me["dp"]

    def rows_for(y):
        return pl.ds(pl.multiple_of(y * quarter, quarter), quarter)

    fold_copies = []
    for i, g in enumerate(group):
        target = moved(me, n, **g)
        fold_copies.append(
            copy_to(
                stage.at[rows_for(target["dp"])], fold.at[slab],
                fold_send.at[i], fold_recv.at[i], target,
            )
        )
        fold_copies[-1].start()
    fold[slab] = stage[rows_for(me["dp"]), :]
    for i in range(len(line)):
        route_copies[i].wait_recv()
    routes_ref[...] = routes[...]
    for f in fold_copies:
        f.wait_recv()
    slabs = fold.shape[0]
    width = stage.shape[1]
    squares = jnp.zeros((quarter, width), f32)
    for s in range(slabs):
        v = fold[s].astype(f32)
        squares += v * v
    squares = jnp.sum(squares, 1, keepdims=True)
    inverse = lax.rsqrt(squares / (slabs * width) + epsilon)
    per_core = slabs // n["core"]
    for i in range(per_core):
        s = core * per_core + i
        gain = gain_ref[:, pl.ds(pl.multiple_of(s * width, width), width)].astype(f32)
        normed_ref[:, i * width : (i + 1) * width] = (
            fold[s].astype(f32) * inverse * gain
        ).astype(bf16)
    for i in range(n["dp"]):
        kept_ref[:, i * width : (i + 1) * width] = fold[tensor * n["dp"] + i]

    for c in z_copies.values():
        c.wait_send()
    for d in range(reach + 1):
        for i in range(len(plane)):
            plane_copy(d, i).wait_send()
        core_copy(d).wait_send()
    for c in route_copies + fold_copies:
        c.wait_send()


def attention_call(q, k, v, segments, resid, gain, ids, gates):
    n = sizes()
    rows, width = q.shape
    plane_rows = n["xh"] * rows
    reach = min(-(-REACH // plane_rows), n["z"] - 1)
    per_plane = n["xh"] * n["dp"]
    experts = per_plane * n["z"]
    lanes = ids.shape[1]
    quarter = rows // n["dp"]
    slabs = n["xl"] * n["core"] * n["dp"]
    dma = pltpu.SemaphoreType.DMA
    return pl.pallas_call(
        functools.partial(attention_kernel, n),
        out_shape=(
            jax.ShapeDtypeStruct((quarter, slabs * width // n["core"]), bf16),
            jax.ShapeDtypeStruct((quarter, n["dp"] * width), bf16),
            jax.ShapeDtypeStruct((n["z"], 2, per_plane, lanes), f32),
        ),
        in_specs=[pl.BlockSpec(memory_space=pltpu.VMEM)] * 8,
        out_specs=(pl.BlockSpec(memory_space=pltpu.VMEM),) * 3,
        scratch_shapes=[
            pltpu.VMEM((2, reach + 1, plane_rows, HEAD_WIDTH), bf16),
            pltpu.VMEM((rows * width // HEAD_WIDTH, HEAD_WIDTH), bf16),
            pltpu.VMEM((2, experts, lanes), f32),
            pltpu.VMEM((n["z"], 2, per_plane, lanes), f32),
            pltpu.VMEM((rows, width), bf16),
            pltpu.VMEM((slabs, quarter, width), bf16),
            dma((reach + 1,)),
            dma((reach + 1,)),
            dma((reach + 1, per_plane)),
            dma((reach + 1, per_plane)),
            dma((reach + 1,)),
            dma((reach + 1,)),
            dma((n["z"],)),
            dma((n["z"],)),
            dma((slabs,)),
            dma((slabs,)),
        ],
        compiler_params=pltpu.CompilerParams(
            collective_id=0, has_side_effects=True, vmem_limit_bytes=32 * 1024 * 1024
        ),
        name="attention",
    )(q, k, v, segments, resid, gain, ids, gates)


def expert_kernel(
    n, normed_ref, kept_ref, routes_ref, gate_hbm, up_hbm, down_hbm,
    mixed_ref,
    w_gate, w_up, w_down, tokens, picked, arrived, hidden, produced, returned, partial,
    fall_out, fall_in, rise_out, rise_in,
    w_sem, up_send, up_recv, down_send, down_recv, pick_send, pick_recv, core_send, core_recv,
    hid_send, hid_recv, ret_send, ret_recv, fall_send, fall_recv, rise_send, rise_recv,
):
    me = places()
    up, down = n["z"] // 2, n["z"] // 2 - 1
    groups = n["z"] // GROUP
    plane = shifts(n, ("xh", "dp"))
    tensor_steps = shifts(n, ("xl", "core"))
    experts = n["xh"] * n["dp"]
    core = me["core"]
    tensor = me["xl"] * n["core"] + core
    mine = me["xh"] * n["dp"] + me["dp"]
    w_copies = [
        pltpu.make_async_copy(a, b, w_sem.at[i])
        for i, (a, b) in enumerate(((gate_hbm, w_gate), (up_hbm, w_up), (down_hbm, w_down)))
    ]
    for c in w_copies:
        c.start()
    tokens[0] = normed_ref[...]
    greet(me, n, [{"z": 1}, {"z": -1}] + plane + tensor_steps)

    def up_copy(k):
        return copy_to(
            tokens.at[up_place(k)], tokens.at[up_place(k + 1)],
            up_send.at[k], up_recv.at[k], moved(me, n, z=1),
        )

    def down_copy(k):
        return copy_to(
            tokens.at[2 * k], tokens.at[2 * k + 2],
            down_send.at[k], down_recv.at[k], moved(me, n, z=-1),
        )

    def pick_copy(g, i):
        to = moved(me, n, **plane[i])
        to_index = to.get("xh", me["xh"]) * n["dp"] + to.get("dp", me["dp"])
        return copy_to(
            picked.at[g, to_index], arrived.at[core, g, mine],
            pick_send.at[g, i], pick_recv.at[g, i], to,
        )

    def core_copy(g, half):
        return copy_to(
            arrived.at[half, g], arrived.at[half, g],
            core_send.at[g], core_recv.at[g], moved(me, n, core=1),
        )

    def hid_copy(g, i):
        return copy_to(
            hidden.at[g, tensor], hidden.at[g, tensor],
            hid_send.at[g, i], hid_recv.at[g, i], moved(me, n, **tensor_steps[i]),
        )

    def ret_copy(g, i):
        back = {a: -s for a, s in plane[i].items()}
        to = moved(me, n, **back)
        to_index = to.get("xh", me["xh"]) * n["dp"] + to.get("dp", me["dp"])
        return copy_to(
            produced.at[g, to_index], returned.at[g, mine],
            ret_send.at[g, i], ret_recv.at[g, i], to,
        )

    def slots_of(g):
        lanes = routes_ref.shape[-1]
        lane = lax.broadcasted_iota(jnp.int32, (experts, lanes), 1)
        rank, weight = routes_ref[GROUP * g, 0], routes_ref[GROUP * g, 1]
        for j in range(1, GROUP):
            own = lane // BLOCK == j
            rank = jnp.where(own, routes_ref[GROUP * g + j, 0], rank)
            weight = jnp.where(own, routes_ref[GROUP * g + j, 1], weight)
        shape = (experts, SLOTS, lanes)
        slot = lax.broadcasted_iota(jnp.int32, shape, 1)
        token = lax.broadcasted_iota(jnp.int32, shape, 2)
        held = (jnp.broadcast_to(rank[:, None, :], shape) == lax.rem(slot, CAP).astype(f32)) & (
            token // BLOCK == slot // CAP
        )
        weight = jnp.where(held, jnp.broadcast_to(weight[:, None, :], shape), 0.0)
        flat = (experts * SLOTS, lanes)
        return jnp.where(held, 1.0, 0.0).reshape(flat), weight.reshape(flat)

    def pick(g):
        chosen, _ = slots_of(g)
        block = tokens[GROUP * g : GROUP * (g + 1)].reshape(GROUP * BLOCK, tokens.shape[2])
        out = jnp.dot(chosen.astype(bf16), block, preferred_element_type=f32).astype(bf16)
        picked[g] = out.reshape(picked.shape[1:])
        for i in range(len(plane)):
            pick_copy(g, i).start()
        arrived[core, g, mine] = picked[g, mine]

    def pass_on(g):
        for i in range(len(plane)):
            pick_copy(g, i).wait_recv()
        core_copy(g, core).start()

    contract = (((1,), (1,)), ((), ()))
    n_slots = experts * SLOTS

    def into_hidden(g):
        core_copy(g, 1 - core).wait_recv()
        gate_val = up_val = None
        half = arrived.shape[-1]
        for h in range(n["core"]):
            x = arrived[h, g].reshape(n_slots, half)
            cols = slice(h * half, (h + 1) * half)
            a = lax.dot_general(x, w_gate[0, :, cols], contract, preferred_element_type=f32)
            b = lax.dot_general(x, w_up[0, :, cols], contract, preferred_element_type=f32)
            gate_val = a if gate_val is None else gate_val + a
            up_val = b if up_val is None else up_val + b
        hidden[g, tensor] = (gate_val / (1.0 + jnp.exp(-gate_val)) * up_val).astype(bf16)
        for i in range(len(tensor_steps)):
            hid_copy(g, i).start()

    def out_of_hidden(g):
        for i in range(len(tensor_steps)):
            hid_copy(g, i).wait_recv()
        units = hidden.shape[-1]
        out = None
        for s in range(hidden.shape[1]):
            term = jnp.dot(
                hidden[g, s], w_down[0, s * units : (s + 1) * units, :], preferred_element_type=f32
            )
            out = term if out is None else out + term
        produced[g] = out.astype(bf16).reshape(produced.shape[1:])
        for i in range(len(plane)):
            ret_copy(g, i).start()
        returned[g, mine] = produced[g, mine]

    def mix(g):
        _, weight = slots_of(g)
        for i in range(len(plane)):
            ret_copy(g, i).wait_recv()
        high = weight.astype(bf16)
        low = (weight - high.astype(f32)).astype(bf16)
        back = returned[g].reshape(n_slots, returned.shape[-1])
        over = (((0,), (0,)), ((), ()))
        total = lax.dot_general(high, back, over, preferred_element_type=f32)
        total += lax.dot_general(low, back, over, preferred_element_type=f32)
        partial[GROUP * g : GROUP * (g + 1)] = total.reshape(GROUP, BLOCK, total.shape[-1])

    up_copy(0).start()
    down_copy(0).start()
    for c in w_copies:
        c.wait()
    for step in range(1, up + 1):
        up_copy(step - 1).wait_recv()
        if step < up:
            up_copy(step).start()
        if step <= down:
            down_copy(step - 1).wait_recv()
            if step < down:
                down_copy(step).start()
        if step % 2:
            continue
        g = step // 2 - 1
        pick(g)
        if g >= 1:
            pass_on(g - 1)
        if g >= 2:
            into_hidden(g - 2)
        if g >= 3:
            out_of_hidden(g - 3)
    for g in range(groups, groups + 3):
        if 0 <= g - 1 < groups:
            pass_on(g - 1)
        if 0 <= g - 2 < groups:
            into_hidden(g - 2)
        if 0 <= g - 3 < groups:
            out_of_hidden(g - 3)

    part_width = partial.shape[-1] // SPLIT

    def piece(k_place, s):
        return partial[k_place, :, s * part_width : (s + 1) * part_width]

    def fall_copy(k, s):
        return copy_to(
            fall_out.at[k - 1, s], fall_in.at[k - 1, s],
            fall_send.at[k - 1, s], fall_recv.at[k - 1, s], moved(me, n, z=-1),
        )

    def rise_copy(k, s):
        return copy_to(
            rise_out.at[k - 1, s], rise_in.at[k - 1, s],
            rise_send.at[k - 1, s], rise_recv.at[k - 1, s], moved(me, n, z=1),
        )

    mixed_groups = set()

    def need(place):
        if place // GROUP not in mixed_groups:
            mixed_groups.add(place // GROUP)
            mix(place // GROUP)

    for t in range(up):
        k, j = up - t, down - t
        need(2 * k - 1)
        for s in range(SPLIT):
            total = piece(2 * k - 1, s)
            if t:
                fall_copy(k + 1, s).wait_recv()
                total = total + fall_in[k, s].astype(f32)
            fall_out[k - 1, s] = total.astype(bf16)
            fall_copy(k, s).start()
        if j < 1:
            continue
        need(2 * j)
        for s in range(SPLIT):
            total = piece(2 * j, s)
            if t:
                rise_copy(j + 1, s).wait_recv()
                total = total + rise_in[j, s].astype(f32)
            rise_out[j - 1, s] = total.astype(bf16)
            rise_copy(j, s).start()
    for s in range(SPLIT):
        cols = slice(s * part_width, (s + 1) * part_width)
        total = kept_ref[:, cols].astype(f32) + piece(0, s)
        if down:
            rise_copy(1, s).wait_recv()
            total += rise_in[0, s].astype(f32)
        fall_copy(1, s).wait_recv()
        mixed_ref[:, cols] = (total + fall_in[0, s].astype(f32)).astype(bf16)

    for k in range(up):
        up_copy(k).wait_send()
    for k in range(down):
        down_copy(k).wait_send()
    for g in range(groups):
        core_copy(g, core).wait_send()
        for i in range(len(plane)):
            pick_copy(g, i).wait_send()
            ret_copy(g, i).wait_send()
        for i in range(len(tensor_steps)):
            hid_copy(g, i).wait_send()
    for s in range(SPLIT):
        for k in range(1, up + 1):
            fall_copy(k, s).wait_send()
        for k in range(1, down + 1):
            rise_copy(k, s).wait_send()


def expert_call(normed, kept, routes, w_gate, w_up, w_down):
    n = sizes()
    up, down = n["z"] // 2, n["z"] // 2 - 1
    groups = n["z"] // GROUP
    experts = n["xh"] * n["dp"]
    tensors = n["xl"] * n["core"]
    half, width = normed.shape[1], kept.shape[1]
    units = w_gate.shape[1]
    n_slots = experts * SLOTS
    part_width = width // SPLIT
    dma = pltpu.SemaphoreType.DMA
    vmem = pl.BlockSpec(memory_space=pltpu.VMEM)
    hbm = pl.BlockSpec(memory_space=pl.ANY)
    return pl.pallas_call(
        functools.partial(expert_kernel, n),
        out_shape=jax.ShapeDtypeStruct((BLOCK, width), bf16),
        in_specs=[vmem] * 3 + [hbm] * 3,
        out_specs=vmem,
        scratch_shapes=[
            pltpu.VMEM(w_gate.shape, bf16),
            pltpu.VMEM(w_up.shape, bf16),
            pltpu.VMEM(w_down.shape, bf16),
            pltpu.VMEM((n["z"], BLOCK, half), bf16),
            pltpu.VMEM((groups, experts, SLOTS, half), bf16),
            pltpu.VMEM((n["core"], groups, experts, SLOTS, half), bf16),
            pltpu.VMEM((groups, tensors, n_slots, units), bf16),
            pltpu.VMEM((groups, experts, SLOTS, width), bf16),
            pltpu.VMEM((groups, experts, SLOTS, width), bf16),
            pltpu.VMEM((n["z"], BLOCK, width), f32),
            pltpu.VMEM((up, SPLIT, BLOCK, part_width), bf16),
            pltpu.VMEM((up, SPLIT, BLOCK, part_width), bf16),
            pltpu.VMEM((max(down, 1), SPLIT, BLOCK, part_width), bf16),
            pltpu.VMEM((max(down, 1), SPLIT, BLOCK, part_width), bf16),
            dma((3,)),
            dma((up,)),
            dma((up,)),
            dma((max(down, 1),)),
            dma((max(down, 1),)),
            dma((groups, experts)),
            dma((groups, experts)),
            dma((groups,)),
            dma((groups,)),
            dma((groups, tensors)),
            dma((groups, tensors)),
            dma((groups, experts)),
            dma((groups, experts)),
            dma((up, SPLIT)),
            dma((up, SPLIT)),
            dma((max(down, 1), SPLIT)),
            dma((max(down, 1), SPLIT)),
        ],
        compiler_params=pltpu.CompilerParams(
            collective_id=1, has_side_effects=True, vmem_limit_bytes=48 * 1024 * 1024
        ),
        name="experts",
    )(normed, kept, routes, w_gate, w_up, w_down)


def body(
    q_proj,
    key_projection,
    value_projection,
    segments,
    resid,
    norm_gain,
    route_ids,
    route_gates,
    w_gate,
    w_up,
    w_down,
):
    normed, kept, routes = attention_call(
        q_proj,
        key_projection,
        value_projection,
        segments.reshape(1, -1),
        resid,
        norm_gain.reshape(1, -1),
        jnp.tile(route_ids.T, (1, GROUP)),
        jnp.tile(route_gates.T, (1, GROUP)),
    )
    return expert_call(normed, kept, routes, w_gate, w_up, w_down)


def solution(mesh):
    n_cp, n_tp, n_dp = (mesh.shape[a] for a in ("cp", "tp", "dp"))
    fine = Mesh(
        mesh.devices.reshape(n_cp // 2, 2, n_tp // 2, 2, n_dp), ("z", "xh", "xl", "core", "dp")
    )
    cp, tp = ("z", "xh"), ("xl", "core")
    placed = (
        P(cp, tp + ("dp",)),
        P(cp, None),
        P(cp, None),
        P(),
        P(cp, tp + ("dp",)),
        P(),
        P(cp + ("dp",), None),
        P(cp + ("dp",), None),
        P(cp + ("dp",), tp, None),
        P(cp + ("dp",), tp, None),
        P(cp + ("dp",), None, tp),
    )
    return jax.shard_map(
        body, mesh=fine, in_specs=placed, out_specs=P(cp + ("dp",), tp), check_vma=False
    )
```

```python
import functools

import jax
import jax.numpy as jnp
from jax import lax
from jax.experimental import pallas as pl
from jax.experimental.pallas import tpu as pltpu
from jax.sharding import Mesh, PartitionSpec as P

HEAD_WIDTH = 128
CAP = 4
REACH = 2048
BLOCK = 32
GROUP = 4
SLOTS = GROUP * CAP
SPLIT = 4
PIECES = 4
FAR_FIRST = True
PAIRED = 4
LAG_CORE, LAG_USE = 3, 2

epsilon = 1e-06
masked_score = -1e30
bf16, f32 = jnp.bfloat16, jnp.float32
MESH = pl.DeviceIdType.MESH


def sizes():
    return {a: lax.axis_size(a) for a in ("z", "xh", "xl", "core", "dp")}


def places():
    return {a: lax.axis_index(a) for a in ("z", "xh", "xl", "core", "dp")}


def moved(me, n, **steps):
    return {a: lax.rem(me[a] + n[a] + s, n[a]) for a, s in steps.items()}


def shifts(n, axes):
    found = [{}]
    for a in axes:
        found = [{**f, a: s} for f in found for s in range(n[a])]
    return found[1:]


def copy_to(src, dst, send, recv, device):
    return pltpu.make_async_remote_copy(
        src_ref=src, dst_ref=dst, send_sem=send, recv_sem=recv, device_id=device, device_id_type=MESH
    )


def greet(me, n, steps):
    barrier = pltpu.get_barrier_semaphore()
    for s in steps:
        pl.semaphore_signal(barrier, inc=1, device_id=moved(me, n, **s), device_id_type=MESH)
    pl.semaphore_wait(barrier, len(steps))


def next_stop(k):
    if k <= PAIRED:
        return k - 1
    return k - 2 if k % 2 == 0 else k - 1


def up_place(k):
    return 2 * k - 1 if k else 0


def layer_kernel(
    n, q_hbm, k_hbm, v_hbm, seg_hbm, resid_hbm, gain_hbm, ids_hbm, gates_hbm, w_gate_hbm, w_up_hbm, w_down_hbm,
    mixed_ref,
    q_ref, k_ref, v_ref, seg_ref, resid_ref, gain_ref, ids_ref, gates_ref, w_gate, w_up, w_down,
    kv, queries, table, routes, stage, fold, kept, wide_gain,
    tokens, picked, arrived, hidden, produced, returned, partial, fall_out, fall_in, rise_out, rise_in,
    in_sem, z_send, z_recv, plane_send, plane_recv, share_send, share_recv,
    route_send, route_recv, fold_send, fold_recv,
    up_send, up_recv, down_send, down_recv, pick_send, pick_recv, core_send, core_recv,
    hid_send, hid_recv, ret_send, ret_recv, fall_send, fall_recv, rise_send, rise_recv,
):
    me = places()
    rows = q_ref.shape[0]
    heads = q_ref.shape[1] // HEAD_WIDTH
    plane_rows = n["xh"] * rows
    reach = min(-(-REACH // plane_rows), n["z"] - 1)
    up, down = n["z"] // 2, n["z"] // 2 - 1
    groups = n["z"] // GROUP
    plane = shifts(n, ("xh", "dp"))
    group = shifts(n, ("xl", "core", "dp"))
    tensor_steps = shifts(n, ("xl", "core"))
    line = [{"z": s} for s in range(1, n["z"])]
    core = me["core"]
    tensor = me["xl"] * n["core"] + core
    mine = me["xh"] * n["dp"] + me["dp"]
    experts = n["xh"] * n["dp"]

    pairs = (
        (k_hbm, k_ref), (v_hbm, v_ref), (ids_hbm, ids_ref), (gates_hbm, gates_ref), (q_hbm, q_ref),
        (seg_hbm, seg_ref), (resid_hbm, resid_ref), (gain_hbm, gain_ref),
        (w_gate_hbm, w_gate), (w_up_hbm, w_up), (w_down_hbm, w_down),
    )
    loads = [pltpu.make_async_copy(a, b, in_sem.at[i]) for i, (a, b) in enumerate(pairs)]
    for c in loads:
        c.start()
    crossed = [{**p, "xl": n["xl"] // 2 if p["xh"] else 0} for p in plane]
    greet(
        me, n,
        line + plane + [g for g in group if g["xl"] or g["core"]] + [p for p in crossed if p["xl"]],
    )

    quarter = rows // n["dp"]
    start = pl.multiple_of(me["xh"] * rows + me["dp"] * quarter, quarter)
    here = pl.ds(start, quarter)
    head = pl.ds(pl.multiple_of(me["xl"] * HEAD_WIDTH, HEAD_WIDTH), HEAD_WIDTH)
    own = pl.ds(pl.multiple_of(me["dp"] * quarter, quarter), quarter)
    loads[0].wait()
    loads[1].wait()
    kv[core, 0, here, :] = jnp.where(core == 0, k_ref[own, head], v_ref[own, head])

    def z_copy(d):
        return copy_to(
            kv.at[core, 0, here], kv.at[core, d, here], z_send.at[d], z_recv.at[d], moved(me, n, z=d)
        )

    def plane_copy(d, i):
        return copy_to(
            kv.at[core, d, here], kv.at[core, d, here],
            plane_send.at[d, i], plane_recv.at[d, i], moved(me, n, **plane[i]),
        )

    def share_copy(d, which):
        return copy_to(
            kv.at[which, d], kv.at[which, d], share_send.at[d], share_recv.at[d], moved(me, n, core=1)
        )

    order = [0] + list(range(reach, 0, -1)) if FAR_FIRST else list(range(reach + 1))
    for d in order[1:]:
        z_copy(d).start()
    for i in range(len(plane)):
        plane_copy(0, i).start()

    lanes = table.shape[2]
    all_experts = table.shape[1]
    token = lax.broadcasted_iota(jnp.int32, (BLOCK, lanes), 0)
    lane = lax.broadcasted_iota(jnp.int32, (BLOCK, lanes), 1)
    spread = jnp.where(lax.rem(lane, BLOCK) == token, 1.0, 0.0)
    over = (((0,), (0,)), ((), ()))
    exact = dict(preferred_element_type=f32, precision=lax.Precision.HIGHEST)
    loads[2].wait()
    loads[3].wait()
    ids = jnp.dot(ids_ref[...].astype(f32), spread, **exact)
    gates = jnp.dot(gates_ref[...], spread, **exact)
    expert = lax.broadcasted_iota(jnp.int32, (all_experts, lanes), 0).astype(f32)
    named = jnp.zeros((all_experts, lanes), f32)
    weight = jnp.zeros((all_experts, lanes), f32)
    for j in range(ids.shape[0]):
        equal = jnp.abs(expert - ids[j : j + 1, :]) < 0.5
        named += jnp.where(equal, 1.0, 0.0)
        weight += jnp.where(equal, gates[j : j + 1, :], 0.0)
    earlier = lax.broadcasted_iota(jnp.int32, (lanes, lanes), 0)
    later = lax.broadcasted_iota(jnp.int32, (lanes, lanes), 1)
    before = (earlier < later) & (earlier // BLOCK == later // BLOCK)
    rank = jnp.dot(
        named.astype(bf16), jnp.where(before, 1.0, 0.0).astype(bf16), preferred_element_type=f32
    )
    table[0] = jnp.where(named > 0.5, rank, 2.0 * CAP)
    table[1] = weight

    def rows_of(plane_index):
        return pl.ds(pl.multiple_of(plane_index * experts, experts), experts)

    route_copies = []
    for k, place in [(k, 2 * k - 1) for k in range(1, up + 1)] + [(-k, 2 * k) for k in range(1, down + 1)]:
        target = moved(me, n, z=k)
        route_copies.append(
            copy_to(
                table.at[:, rows_of(target["z"])], routes.at[place],
                route_send.at[place], route_recv.at[place], target,
            )
        )
    routes[0] = table[:, rows_of(me["z"]), :]

    for c in loads[4:8]:
        c.wait()
    wide_gain[...] = gain_ref[...].astype(f32)
    for h in range(heads):
        queries[h * rows : (h + 1) * rows] = q_ref[:, h * HEAD_WIDTH : (h + 1) * HEAD_WIDTH]
    all_rows = heads * rows
    context = me["z"] * n["xh"] + me["xh"]
    first_row = pl.multiple_of(context * rows, rows)
    seg_here = seg_ref[:, pl.ds(first_row, rows)].astype(f32)
    r = lax.broadcasted_iota(jnp.int32, (all_rows, rows), 0)
    c = lax.broadcasted_iota(jnp.int32, (all_rows, rows), 1)
    seg_rows = jnp.sum(jnp.where(lax.rem(r, rows) == c, seg_here, 0.0), 1, keepdims=True)
    q_position = first_row + lax.rem(
        lax.broadcasted_iota(jnp.int32, (all_rows, plane_rows), 0), rows
    )
    k_offset = lax.broadcasted_iota(jnp.int32, (all_rows, plane_rows), 1)
    state = None
    for t in range(len(order) + LAG_CORE + LAG_USE):
        if 1 <= t < len(order):
            z_copy(order[t]).wait_recv()
            for i in range(len(plane)):
                plane_copy(order[t], i).start()
            if t == len(order) - 1:
                for copy in route_copies:
                    copy.start()
        if 0 <= t - LAG_CORE < len(order):
            for i in range(len(plane)):
                plane_copy(order[t - LAG_CORE], i).wait_recv()
            share_copy(order[t - LAG_CORE], core).start()
        if t < LAG_CORE + LAG_USE:
            continue
        d = order[t - LAG_CORE - LAG_USE]
        share_copy(d, 1 - core).wait_recv()
        first_key = pl.multiple_of(lax.rem(me["z"] + n["z"] - d, n["z"]) * plane_rows, plane_rows)
        scores = (
            lax.dot_general(
                queries[...], kv[0, d], (((1,), (1,)), ((), ())), preferred_element_type=f32
            )
            * HEAD_WIDTH ** (-0.5)
        )
        seg_keys = seg_ref[:, pl.ds(first_key, plane_rows)].astype(f32)
        allowed = (first_key + k_offset <= q_position) & (seg_keys == seg_rows)
        scores = jnp.where(allowed, scores, masked_score)
        top = jnp.max(scores, 1, keepdims=True)
        if state is None:
            weights = jnp.exp(scores - top)
            total = jnp.sum(weights, 1, keepdims=True)
            acc = jnp.dot(weights.astype(bf16), kv[1, d], preferred_element_type=f32)
        else:
            old_top, old_total, old_acc = state
            top = jnp.maximum(old_top, top)
            weights = jnp.exp(scores - top)
            fade = jnp.exp(old_top - top)
            total = old_total * fade + jnp.sum(weights, 1, keepdims=True)
            acc = old_acc * fade + jnp.dot(
                weights.astype(bf16), kv[1, d], preferred_element_type=f32
            )
        state = (top, total, acc)
    attended = state[2] / state[1]
    for h in range(heads):
        cols = slice(h * HEAD_WIDTH, (h + 1) * HEAD_WIDTH)
        stage[:, cols] = (
            resid_ref[:, cols].astype(f32) + attended[h * rows : (h + 1) * rows]
        ).astype(bf16)

    slab = tensor * n["dp"] + me["dp"]

    def rows_for(y):
        return pl.ds(pl.multiple_of(y * quarter, quarter), quarter)

    fold_copies = []
    for i, g in enumerate(group):
        target = moved(me, n, **g)
        fold_copies.append(
            copy_to(
                stage.at[rows_for(target["dp"])], fold.at[slab],
                fold_send.at[i], fold_recv.at[i], target,
            )
        )
        fold_copies[-1].start()
    fold[slab] = stage[rows_for(me["dp"]), :]
    for f in route_copies + fold_copies:
        f.wait_recv()
    slabs = fold.shape[0]
    width = stage.shape[1]
    squares = jnp.zeros((quarter, width), f32)
    for s in range(slabs):
        v = fold[s].astype(f32)
        squares += v * v
    squares = jnp.sum(squares, 1, keepdims=True)
    inverse = lax.rsqrt(squares / (slabs * width) + epsilon)
    per_core = slabs // n["core"]
    piece_width = tokens.shape[3]

    def up_copy(k, p):
        return copy_to(
            tokens.at[up_place(k), p], tokens.at[up_place(k + 1), p],
            up_send.at[k, p], up_recv.at[k, p], moved(me, n, z=1),
        )

    def down_copy(k, p):
        return copy_to(
            tokens.at[2 * k, p], tokens.at[2 * k + 2, p],
            down_send.at[k, p], down_recv.at[k, p], moved(me, n, z=-1),
        )

    for i in range(per_core):
        s = core * per_core + i
        lines = [wide_gain[pl.ds(s * (width // 128) + r, 1), :] for r in range(width // 128)]
        gain = jnp.concatenate(lines, 1)
        p, q = divmod(i * width, piece_width)
        tokens[0, p, :, q : q + width] = (fold[s].astype(f32) * inverse * gain).astype(bf16)
        if q + width == piece_width:
            up_copy(0, p).start()
            down_copy(0, p).start()
    for i in range(n["dp"]):
        kept[:, i * width : (i + 1) * width] = fold[tensor * n["dp"] + i]

    def pick_copy(g, i):
        to = moved(me, n, **crossed[i])
        return copy_to(
            picked.at[g, to["xh"] * n["dp"] + to["dp"]], arrived.at[core, g, mine],
            pick_send.at[g, i], pick_recv.at[g, i], to,
        )

    def core_copy(g, half):
        return copy_to(
            arrived.at[half, g], arrived.at[half, g],
            core_send.at[g], core_recv.at[g], moved(me, n, core=1),
        )

    def hid_copy(g, i):
        return copy_to(
            hidden.at[g, tensor], hidden.at[g, tensor],
            hid_send.at[g, i], hid_recv.at[g, i], moved(me, n, **tensor_steps[i]),
        )

    def ret_copy(g, i):
        to = moved(me, n, **{a: -s for a, s in plane[i].items()})
        return copy_to(
            produced.at[g, to["xh"] * n["dp"] + to["dp"]], returned.at[g, mine],
            ret_send.at[g, i], ret_recv.at[g, i], to,
        )

    def slots_of(g):
        lane = lax.broadcasted_iota(jnp.int32, (experts, lanes), 1)
        rank, weight = routes[GROUP * g, 0], routes[GROUP * g, 1]
        for j in range(1, GROUP):
            inside = lane // BLOCK == j
            rank = jnp.where(inside, routes[GROUP * g + j, 0], rank)
            weight = jnp.where(inside, routes[GROUP * g + j, 1], weight)
        shape = (experts, SLOTS, lanes)
        slot = lax.broadcasted_iota(jnp.int32, shape, 1)
        token = lax.broadcasted_iota(jnp.int32, shape, 2)
        held = (jnp.broadcast_to(rank[:, None, :], shape) == lax.rem(slot, CAP).astype(f32)) & (
            token // BLOCK == slot // CAP
        )
        weight = jnp.where(held, jnp.broadcast_to(weight[:, None, :], shape), 0.0)
        flat = (experts * SLOTS, lanes)
        return jnp.where(held, 1.0, 0.0).reshape(flat), weight.reshape(flat)

    def pick(g):
        chosen, _ = slots_of(g)
        chosen = chosen.astype(bf16)
        for p in range(PIECES):
            block = tokens[GROUP * g : GROUP * (g + 1), p].reshape(GROUP * BLOCK, piece_width)
            out = jnp.dot(chosen, block, preferred_element_type=f32).astype(bf16)
            picked[g, :, :, p * piece_width : (p + 1) * piece_width] = out.reshape(
                experts, SLOTS, piece_width
            )
        for i in range(len(plane)):
            pick_copy(g, i).start()
        arrived[core, g, mine] = picked[g, mine]

    def pass_on(g):
        for i in range(len(plane)):
            pick_copy(g, i).wait_recv()
        core_copy(g, core).start()

    contract = (((1,), (1,)), ((), ()))
    n_slots = experts * SLOTS

    def into_hidden(g):
        core_copy(g, 1 - core).wait_recv()
        gate_val = up_val = None
        half = arrived.shape[-1]
        for h in range(n["core"]):
            x = arrived[h, g].reshape(n_slots, half)
            cols = slice(h * half, (h + 1) * half)
            a = lax.dot_general(x, w_gate[0, :, cols], contract, preferred_element_type=f32)
            b = lax.dot_general(x, w_up[0, :, cols], contract, preferred_element_type=f32)
            gate_val = a if gate_val is None else gate_val + a
            up_val = b if up_val is None else up_val + b
        hidden[g, tensor] = (gate_val / (1.0 + jnp.exp(-gate_val)) * up_val).astype(bf16)
        for i in range(len(tensor_steps)):
            hid_copy(g, i).start()

    def out_of_hidden(g):
        for i in range(len(tensor_steps)):
            hid_copy(g, i).wait_recv()
        units = hidden.shape[-1]
        out = None
        for s in range(hidden.shape[1]):
            term = jnp.dot(
                hidden[g, s], w_down[0, s * units : (s + 1) * units, :], preferred_element_type=f32
            )
            out = term if out is None else out + term
        produced[g] = out.astype(bf16).reshape(produced.shape[1:])
        for i in range(len(plane)):
            ret_copy(g, i).start()
        returned[g, mine] = produced[g, mine]

    def mix(g):
        _, weight = slots_of(g)
        for i in range(len(plane)):
            ret_copy(g, i).wait_recv()
        high = weight.astype(bf16)
        low = (weight - high.astype(f32)).astype(bf16)
        back = returned[g].reshape(n_slots, returned.shape[-1])
        total = lax.dot_general(high, back, over, preferred_element_type=f32)
        total += lax.dot_general(low, back, over, preferred_element_type=f32)
        partial[GROUP * g : GROUP * (g + 1)] = total.reshape(GROUP, BLOCK, total.shape[-1])

    for c in loads[8:]:
        c.wait()
    agenda = []
    for g in range(groups):
        for delay, rank, act in ((2, 0, pick), (4, 1, pass_on), (7, 2, out_of_hidden), (5, 3, into_hidden)):
            agenda.append((2 * g + delay, rank, g, act))
    agenda.sort(key=lambda entry: entry[:3])

    def run(step):
        while agenda and (step is None or agenda[0][0] <= step):
            _, _, g, act = agenda.pop(0)
            act(g)

    for step in range(1, up + 1):
        for p in range(PIECES):
            up_copy(step - 1, p).wait_recv()
            if step < up:
                up_copy(step, p).start()
            if step <= down:
                down_copy(step - 1, p).wait_recv()
                if step < down:
                    down_copy(step, p).start()
        run(step)
    run(None)

    part_width = partial.shape[-1] // SPLIT

    def part(place, s):
        return partial[place, :, s * part_width : (s + 1) * part_width]

    def fall_copy(k, s):
        return copy_to(
            fall_out.at[k - 1, s], fall_in.at[k - 1, s],
            fall_send.at[k - 1, s], fall_recv.at[k - 1, s], moved(me, n, z=next_stop(k) - k),
        )

    def rise_copy(k, s):
        return copy_to(
            rise_out.at[k - 1, s], rise_in.at[k - 1, s],
            rise_send.at[k - 1, s], rise_recv.at[k - 1, s], moved(me, n, z=k - next_stop(k)),
        )

    mixed_groups = set()

    def need(place):
        if place // GROUP not in mixed_groups:
            mixed_groups.add(place // GROUP)
            mix(place // GROUP)

    def gathered(total, k, s, copy, buffer, farthest):
        for other in range(k + 1, farthest + 1):
            if next_stop(other) == k:
                copy(other, s).wait_recv()
                total = total + buffer[other - 1, s].astype(f32)
        return total

    for t in range(up):
        k, j = up - t, down - t
        need(2 * k - 1)
        if j >= 1:
            need(2 * j)
        for s in range(SPLIT):
            fall_out[k - 1, s] = gathered(part(2 * k - 1, s), k, s, fall_copy, fall_in, up).astype(bf16)
            fall_copy(k, s).start()
            if j >= 1:
                rise_out[j - 1, s] = gathered(part(2 * j, s), j, s, rise_copy, rise_in, down).astype(bf16)
                rise_copy(j, s).start()
        if t == 0:
            for g in range(groups - 1, -1, -1):
                need(GROUP * g)
    for s in range(SPLIT):
        cols = slice(s * part_width, (s + 1) * part_width)
        total = kept[:, cols].astype(f32) + part(0, s)
        total = gathered(total, 0, s, rise_copy, rise_in, down)
        mixed_ref[:, cols] = gathered(total, 0, s, fall_copy, fall_in, up).astype(bf16)

    for d in order:
        if d:
            z_copy(d).wait_send()
        for i in range(len(plane)):
            plane_copy(d, i).wait_send()
        share_copy(d, core).wait_send()
    for c in route_copies + fold_copies:
        c.wait_send()
    for p in range(PIECES):
        for k in range(up):
            up_copy(k, p).wait_send()
        for k in range(down):
            down_copy(k, p).wait_send()
    for g in range(groups):
        core_copy(g, core).wait_send()
        for i in range(len(plane)):
            pick_copy(g, i).wait_send()
            ret_copy(g, i).wait_send()
        for i in range(len(tensor_steps)):
            hid_copy(g, i).wait_send()
    for s in range(SPLIT):
        for k in range(1, up + 1):
            fall_copy(k, s).wait_send()
        for k in range(1, down + 1):
            rise_copy(k, s).wait_send()


def body(
    q_proj,
    key_projection,
    value_projection,
    segments,
    resid,
    norm_gain,
    route_ids,
    route_gates,
    w_gate,
    w_up,
    w_down,
):
    n = sizes()
    rows, width = q_proj.shape
    plane_rows = n["xh"] * rows
    reach = min(-(-REACH // plane_rows), n["z"] - 1)
    experts = n["xh"] * n["dp"]
    tensors = n["xl"] * n["core"]
    lanes = GROUP * BLOCK
    slabs = tensors * n["dp"]
    up, down = n["z"] // 2, max(n["z"] // 2 - 1, 1)
    groups = n["z"] // GROUP
    half = slabs * width // n["core"]
    out_width = n["dp"] * width
    units = w_gate.shape[1]
    n_slots = experts * SLOTS
    part_width = out_width // SPLIT
    args = (
        q_proj, key_projection, value_projection, segments.reshape(1, -1), resid, norm_gain.reshape(-1, 128),
        route_ids.T, route_gates.T, w_gate, w_up, w_down,
    )
    held = (0, 1, 2, 3, 4, 5, 6, 7, 8, 9, 10)
    buffers = [
        ((2, reach + 1, plane_rows, HEAD_WIDTH), bf16),
        ((rows * width // HEAD_WIDTH, HEAD_WIDTH), bf16),
        ((2, experts * n["z"], lanes), f32),
        ((n["z"], 2, experts, lanes), f32),
        ((rows, width), bf16),
        ((slabs, BLOCK, width), bf16),
        ((BLOCK, out_width), bf16),
        ((slabs * width // 128, 128), f32),
        ((n["z"], PIECES, BLOCK, half // PIECES), bf16),
        ((groups, experts, SLOTS, half), bf16),
        ((n["core"], groups, experts, SLOTS, half), bf16),
        ((groups, tensors, n_slots, units), bf16),
        ((groups, experts, SLOTS, out_width), bf16),
        ((groups, experts, SLOTS, out_width), bf16),
        ((n["z"], BLOCK, out_width), f32),
        ((up, SPLIT, BLOCK, part_width), bf16),
        ((up, SPLIT, BLOCK, part_width), bf16),
        ((down, SPLIT, BLOCK, part_width), bf16),
        ((down, SPLIT, BLOCK, part_width), bf16),
    ]
    semaphores = [
        (reach + 1,), (reach + 1, experts), (reach + 1,), (n["z"],), (slabs,),
        (up, PIECES), (down, PIECES), (groups, experts), (groups,), (groups, tensors), (groups, experts),
        (up, SPLIT), (down, SPLIT),
    ]
    dma = pltpu.SemaphoreType.DMA
    return pl.pallas_call(
        functools.partial(layer_kernel, n),
        out_shape=jax.ShapeDtypeStruct((BLOCK, out_width), bf16),
        in_specs=[pl.BlockSpec(memory_space=pl.ANY)] * len(args),
        out_specs=pl.BlockSpec(memory_space=pltpu.VMEM),
        scratch_shapes=[pltpu.VMEM(args[i].shape, args[i].dtype) for i in held]
        + [pltpu.VMEM(*b) for b in buffers]
        + [dma((len(args),))]
        + [dma(shape) for shape in semaphores for _ in range(2)],
        compiler_params=pltpu.CompilerParams(
            collective_id=0, has_side_effects=True, vmem_limit_bytes=56 * 1024 * 1024
        ),
        name="layer",
    )(*args)


def solution(mesh):
    n_cp, n_tp, n_dp = (mesh.shape[a] for a in ("cp", "tp", "dp"))
    fine = Mesh(
        mesh.devices.reshape(n_cp // 2, 2, n_tp // 2, 2, n_dp), ("z", "xh", "xl", "core", "dp")
    )
    cp, tp = ("z", "xh"), ("xl", "core")
    placed = (
        P(cp, tp + ("dp",)),
        P(cp, None),
        P(cp, None),
        P(),
        P(cp, tp + ("dp",)),
        P(),
        P(cp + ("dp",), None),
        P(cp + ("dp",), None),
        P(cp + ("dp",), tp, None),
        P(cp + ("dp",), tp, None),
        P(cp + ("dp",), None, tp),
    )
    return jax.shard_map(
        body, mesh=fine, in_specs=placed, out_specs=P(cp + ("dp",), tp), check_vma=False
    )
```

```python
import functools

import jax
import jax.numpy as jnp
from jax import lax
from jax.experimental import pallas as pl
from jax.experimental.pallas import tpu as pltpu
from jax.sharding import Mesh, PartitionSpec as P

HEAD_WIDTH = 128
CAP = 4
REACH = 2048
BLOCK = 32
GROUP = 4
SLOTS = GROUP * CAP
SPLIT = 4
PIECES = 4
PAIRED = 4
LAG_CORE, LAG_USE = 5, 2

epsilon = 1e-06
masked_score = -1e30
bf16, f32 = jnp.bfloat16, jnp.float32
MESH = pl.DeviceIdType.MESH


def sizes():
    return {a: lax.axis_size(a) for a in ("z", "xh", "xl", "core", "dp")}


def places():
    return {a: lax.axis_index(a) for a in ("z", "xh", "xl", "core", "dp")}


def moved(me, n, **steps):
    return {a: lax.rem(me[a] + n[a] + s, n[a]) for a, s in steps.items()}


def shifts(n, axes):
    found = [{}]
    for a in axes:
        found = [{**f, a: s} for f in found for s in range(n[a])]
    return found[1:]


def copy_to(src, dst, send, recv, device):
    return pltpu.make_async_remote_copy(
        src_ref=src, dst_ref=dst, send_sem=send, recv_sem=recv, device_id=device, device_id_type=MESH
    )


def greet(me, n, steps):
    barrier = pltpu.get_barrier_semaphore()
    for s in steps:
        pl.semaphore_signal(barrier, inc=1, device_id=moved(me, n, **s), device_id_type=MESH)
    return lambda: pl.semaphore_wait(barrier, len(steps))


def next_stop(k):
    if k <= PAIRED:
        return k - 1
    return k - 2 if k % 2 == 0 else k - 1


def up_place(k):
    return 2 * k - 1 if k else 0


def layer_kernel(
    n, q_hbm, k_hbm, v_hbm, seg_hbm, resid_hbm, gain_hbm, ids_hbm, gates_hbm, w_gate_hbm, w_up_hbm, w_down_hbm,
    mixed_ref,
    q_ref, k_ref, v_ref, seg_ref, resid_ref, gain_ref, ids_ref, gates_ref, w_gate, w_up, w_down,
    kv, queries, notes, mixer, stage, fold, kept, wide_gain,
    tokens, picked, arrived, hidden, produced, returned, partial, fall_out, fall_in, rise_out, rise_in,
    in_sem, z_send, z_recv, plane_send, plane_recv, share_send, share_recv,
    note_up_send, note_up_recv, note_down_send, note_down_recv, fold_send, fold_recv,
    up_send, up_recv, down_send, down_recv, pick_send, pick_recv, core_send, core_recv,
    hid_send, hid_recv, ret_send, ret_recv, fall_send, fall_recv, rise_send, rise_recv,
):
    me = places()
    rows = q_ref.shape[0]
    heads = q_ref.shape[1] // HEAD_WIDTH
    plane_rows = n["xh"] * rows
    reach = min(-(-REACH // plane_rows), n["z"] - 1)
    up, down = n["z"] // 2, n["z"] // 2 - 1
    groups = n["z"] // GROUP
    plane = shifts(n, ("xh", "dp"))
    group = shifts(n, ("xl", "core", "dp"))
    tensor_steps = shifts(n, ("xl", "core"))
    near = -(-reach // 2)
    stride = max(near, 2 if PAIRED < up else 1)
    line = [{"z": s} for s in range(1, n["z"]) if min(s, n["z"] - s) <= stride]
    core = me["core"]
    tensor = me["xl"] * n["core"] + core
    mine = me["xh"] * n["dp"] + me["dp"]
    experts = n["xh"] * n["dp"]

    crossed = [{**p, "xl": n["xl"] // 2 if p["xh"] else 0} for p in plane]
    met = greet(
        me, n,
        line + plane + [g for g in group if g["xl"] or g["core"]] + [p for p in crossed if p["xl"]],
    )
    pairs = (
        (k_hbm, k_ref), (v_hbm, v_ref), (ids_hbm, ids_ref), (gates_hbm, gates_ref), (q_hbm, q_ref),
        (seg_hbm, seg_ref), (resid_hbm, resid_ref), (gain_hbm, gain_ref),
        (w_gate_hbm, w_gate), (w_up_hbm, w_up), (w_down_hbm, w_down),
    )
    loads = [pltpu.make_async_copy(a, b, in_sem.at[i]) for i, (a, b) in enumerate(pairs)]
    for c in loads:
        c.start()
    met()

    quarter = rows // n["dp"]
    start = pl.multiple_of(me["xh"] * rows + me["dp"] * quarter, quarter)
    here = pl.ds(start, quarter)
    head = pl.ds(pl.multiple_of(me["xl"] * HEAD_WIDTH, HEAD_WIDTH), HEAD_WIDTH)
    own = pl.ds(pl.multiple_of(me["dp"] * quarter, quarter), quarter)
    loads[0].wait()
    loads[1].wait()
    kv[core, 0, here, :] = jnp.where(core == 0, k_ref[own, head], v_ref[own, head])

    def z_copy(d):
        first = 0 if d <= near else near
        return copy_to(
            kv.at[core, first, here], kv.at[core, d, here],
            z_send.at[d], z_recv.at[d], moved(me, n, z=d - first),
        )

    def plane_copy(d, i):
        return copy_to(
            kv.at[core, d, here], kv.at[core, d, here],
            plane_send.at[d, i], plane_recv.at[d, i], moved(me, n, **plane[i]),
        )

    def share_copy(d, which):
        return copy_to(
            kv.at[which, d], kv.at[which, d], share_send.at[d], share_recv.at[d], moved(me, n, core=1)
        )

    order = [0, near] + [d for d in range(1, reach + 1) if d != near]
    for d in order[1 : near + 1]:
        z_copy(d).start()
    for i in range(len(plane)):
        plane_copy(0, i).start()

    lanes = notes.shape[-1]
    token = lax.broadcasted_iota(jnp.int32, (BLOCK, lanes), 0)
    lane = lax.broadcasted_iota(jnp.int32, (BLOCK, lanes), 1)
    spread = jnp.where(lax.rem(lane, BLOCK) == token, 1.0, 0.0)
    over = (((0,), (0,)), ((), ()))
    exact = dict(preferred_element_type=f32, precision=lax.Precision.HIGHEST)
    loads[2].wait()
    loads[3].wait()
    notes[0, 0] = jnp.dot(ids_ref[...].astype(f32), spread, **exact)
    notes[0, 1] = jnp.dot(gates_ref[...], spread, **exact)

    def note_up(k):
        return copy_to(
            notes.at[up_place(k)], notes.at[up_place(k + 1)],
            note_up_send.at[k], note_up_recv.at[k], moved(me, n, z=1),
        )

    def note_down(k):
        return copy_to(
            notes.at[2 * k], notes.at[2 * k + 2],
            note_down_send.at[k], note_down_recv.at[k], moved(me, n, z=-1),
        )

    note_up(0).start()
    note_down(0).start()

    for c in loads[4:8]:
        c.wait()
    wide_gain[...] = gain_ref[...].astype(f32)
    for h in range(heads):
        queries[h * rows : (h + 1) * rows] = q_ref[:, h * HEAD_WIDTH : (h + 1) * HEAD_WIDTH]
    all_rows = heads * rows
    context = me["z"] * n["xh"] + me["xh"]
    first_row = pl.multiple_of(context * rows, rows)
    seg_here = seg_ref[:, pl.ds(first_row, rows)].astype(f32)
    r = lax.broadcasted_iota(jnp.int32, (all_rows, rows), 0)
    c = lax.broadcasted_iota(jnp.int32, (all_rows, rows), 1)
    seg_rows = jnp.sum(jnp.where(lax.rem(r, rows) == c, seg_here, 0.0), 1, keepdims=True)
    q_position = first_row + lax.rem(
        lax.broadcasted_iota(jnp.int32, (all_rows, plane_rows), 0), rows
    )
    k_offset = lax.broadcasted_iota(jnp.int32, (all_rows, plane_rows), 1)
    state = None
    for t in range(len(order) + LAG_CORE + LAG_USE):
        if 1 <= t < len(order):
            z_copy(order[t]).wait_recv()
            if order[t] == near:
                for d in range(near + 1, reach + 1):
                    z_copy(d).start()
            for i in range(len(plane)):
                plane_copy(order[t], i).start()
        if 0 <= t - LAG_CORE < len(order):
            for i in range(len(plane)):
                plane_copy(order[t - LAG_CORE], i).wait_recv()
            share_copy(order[t - LAG_CORE], core).start()
        if t < LAG_CORE + LAG_USE:
            continue
        d = order[t - LAG_CORE - LAG_USE]
        share_copy(d, 1 - core).wait_recv()
        first_key = pl.multiple_of(lax.rem(me["z"] + n["z"] - d, n["z"]) * plane_rows, plane_rows)
        scores = (
            lax.dot_general(
                queries[...], kv[0, d], (((1,), (1,)), ((), ())), preferred_element_type=f32
            )
            * HEAD_WIDTH ** (-0.5)
        )
        seg_keys = seg_ref[:, pl.ds(first_key, plane_rows)].astype(f32)
        allowed = (first_key + k_offset <= q_position) & (seg_keys == seg_rows)
        scores = jnp.where(allowed, scores, masked_score)
        top = jnp.max(scores, 1, keepdims=True)
        if state is None:
            weights = jnp.exp(scores - top)
            total = jnp.sum(weights, 1, keepdims=True)
            acc = jnp.dot(weights.astype(bf16), kv[1, d], preferred_element_type=f32)
        else:
            old_top, old_total, old_acc = state
            top = jnp.maximum(old_top, top)
            weights = jnp.exp(scores - top)
            fade = jnp.exp(old_top - top)
            total = old_total * fade + jnp.sum(weights, 1, keepdims=True)
            acc = old_acc * fade + jnp.dot(
                weights.astype(bf16), kv[1, d], preferred_element_type=f32
            )
        state = (top, total, acc)
    attended = state[2] / state[1]
    for h in range(heads):
        cols = slice(h * HEAD_WIDTH, (h + 1) * HEAD_WIDTH)
        stage[:, cols] = (
            resid_ref[:, cols].astype(f32) + attended[h * rows : (h + 1) * rows]
        ).astype(bf16)

    slab = tensor * n["dp"] + me["dp"]

    def rows_for(y):
        return pl.ds(pl.multiple_of(y * quarter, quarter), quarter)

    fold_copies = []
    for i, g in enumerate(group):
        target = moved(me, n, **g)
        fold_copies.append(
            copy_to(
                stage.at[rows_for(target["dp"])], fold.at[slab],
                fold_send.at[i], fold_recv.at[i], target,
            )
        )
        fold_copies[-1].start()
    fold[slab] = stage[rows_for(me["dp"]), :]
    for f in fold_copies:
        f.wait_recv()
    slabs = fold.shape[0]
    width = stage.shape[1]
    squares = jnp.zeros((quarter, width), f32)
    for s in range(slabs):
        v = fold[s].astype(f32)
        squares += v * v
    squares = jnp.sum(squares, 1, keepdims=True)
    inverse = lax.rsqrt(squares / (slabs * width) + epsilon)
    per_core = slabs // n["core"]
    piece_width = tokens.shape[3]

    def up_copy(k, p):
        return copy_to(
            tokens.at[up_place(k), p], tokens.at[up_place(k + 1), p],
            up_send.at[k, p], up_recv.at[k, p], moved(me, n, z=1),
        )

    def down_copy(k, p):
        return copy_to(
            tokens.at[2 * k, p], tokens.at[2 * k + 2, p],
            down_send.at[k, p], down_recv.at[k, p], moved(me, n, z=-1),
        )

    for i in range(per_core):
        s = core * per_core + i
        lines = [wide_gain[pl.ds(s * (width // 128) + r, 1), :] for r in range(width // 128)]
        gain = jnp.concatenate(lines, 1)
        p, q = divmod(i * width, piece_width)
        tokens[0, p, :, q : q + width] = (fold[s].astype(f32) * inverse * gain).astype(bf16)
        if q + width == piece_width:
            up_copy(0, p).start()
            down_copy(0, p).start()
    for i in range(n["dp"]):
        kept[:, i * width : (i + 1) * width] = fold[tensor * n["dp"] + i]

    def pick_copy(g, i):
        to = moved(me, n, **crossed[i])
        return copy_to(
            picked.at[g, to["xh"] * n["dp"] + to["dp"]], arrived.at[core, g, mine],
            pick_send.at[g, i], pick_recv.at[g, i], to,
        )

    def core_copy(g, half):
        return copy_to(
            arrived.at[half, g], arrived.at[half, g],
            core_send.at[g], core_recv.at[g], moved(me, n, core=1),
        )

    def hid_copy(g, i):
        return copy_to(
            hidden.at[g, tensor], hidden.at[g, tensor],
            hid_send.at[g, i], hid_recv.at[g, i], moved(me, n, **tensor_steps[i]),
        )

    def ret_copy(g, i):
        to = moved(me, n, **{a: -s for a, s in plane[i].items()})
        return copy_to(
            produced.at[g, to["xh"] * n["dp"] + to["dp"]], returned.at[g, mine],
            ret_send.at[g, i], ret_recv.at[g, i], to,
        )

    def slots_of(g):
        row = lax.broadcasted_iota(jnp.int32, (lanes, lanes), 0)
        column = lax.broadcasted_iota(jnp.int32, (lanes, lanes), 1)
        before = (row < column) & (row // BLOCK == column // BLOCK)
        lane = lax.broadcasted_iota(jnp.int32, notes.shape[2:], 1)
        ids, gates = notes[GROUP * g, 0], notes[GROUP * g, 1]
        for j in range(1, GROUP):
            inside = lane // BLOCK == j
            ids = jnp.where(inside, notes[GROUP * g + j, 0], ids)
            gates = jnp.where(inside, notes[GROUP * g + j, 1], gates)
        expert = me["z"] * experts + lax.broadcasted_iota(jnp.int32, (experts, lanes), 0)
        expert = expert.astype(f32)
        named = jnp.zeros((experts, lanes), f32)
        weight = jnp.zeros((experts, lanes), f32)
        for j in range(ids.shape[0]):
            equal = jnp.abs(expert - ids[j : j + 1, :]) < 0.5
            named += jnp.where(equal, 1.0, 0.0)
            weight += jnp.where(equal, gates[j : j + 1, :], 0.0)
        rank = jnp.dot(
            named.astype(bf16), jnp.where(before, 1.0, 0.0).astype(bf16), preferred_element_type=f32
        )
        rank = jnp.where(named > 0.5, rank, 2.0 * CAP)
        shape = (experts, SLOTS, lanes)
        slot = lax.broadcasted_iota(jnp.int32, shape, 1)
        token = lax.broadcasted_iota(jnp.int32, shape, 2)
        held = (jnp.broadcast_to(rank[:, None, :], shape) == lax.rem(slot, CAP).astype(f32)) & (
            token // BLOCK == slot // CAP
        )
        weight = jnp.where(held, jnp.broadcast_to(weight[:, None, :], shape), 0.0)
        flat = (experts * SLOTS, lanes)
        return jnp.where(held, 1.0, 0.0).reshape(flat), weight.reshape(flat)

    def pick(g):
        chosen, mixer[g] = slots_of(g)
        chosen = chosen.astype(bf16)
        for p in range(PIECES):
            block = tokens[GROUP * g : GROUP * (g + 1), p].reshape(GROUP * BLOCK, piece_width)
            out = jnp.dot(chosen, block, preferred_element_type=f32).astype(bf16)
            picked[g, :, :, p * piece_width : (p + 1) * piece_width] = out.reshape(
                experts, SLOTS, piece_width
            )
        for i in range(len(plane)):
            pick_copy(g, i).start()
        arrived[core, g, mine] = picked[g, mine]

    def pass_on(g):
        for i in range(len(plane)):
            pick_copy(g, i).wait_recv()
        core_copy(g, core).start()

    contract = (((1,), (1,)), ((), ()))
    n_slots = experts * SLOTS

    def into_hidden(g):
        core_copy(g, 1 - core).wait_recv()
        gate_val = up_val = None
        half = arrived.shape[-1]
        for h in range(n["core"]):
            x = arrived[h, g].reshape(n_slots, half)
            cols = slice(h * half, (h + 1) * half)
            a = lax.dot_general(w_gate[0, :, cols], x, contract, preferred_element_type=f32)
            b = lax.dot_general(w_up[0, :, cols], x, contract, preferred_element_type=f32)
            gate_val = a if gate_val is None else gate_val + a
            up_val = b if up_val is None else up_val + b
        hidden[g, tensor] = (gate_val / (1.0 + jnp.exp(-gate_val)) * up_val).astype(bf16)
        for i in range(len(tensor_steps)):
            hid_copy(g, i).start()

    def out_of_hidden(g):
        for i in range(len(tensor_steps)):
            hid_copy(g, i).wait_recv()
        units = hidden[g].reshape(w_down.shape[1], n_slots)
        out = lax.dot_general(units, w_down[0], over, preferred_element_type=f32)
        produced[g] = out.astype(bf16).reshape(produced.shape[1:])
        for i in range(len(plane)):
            ret_copy(g, i).start()
        returned[g, mine] = produced[g, mine]

    def mix(g):
        weight = mixer[g]
        for i in range(len(plane)):
            ret_copy(g, i).wait_recv()
        high = weight.astype(bf16)
        low = (weight - high.astype(f32)).astype(bf16)
        back = returned[g].reshape(n_slots, returned.shape[-1])
        total = lax.dot_general(high, back, over, preferred_element_type=f32)
        total += lax.dot_general(low, back, over, preferred_element_type=f32)
        partial[GROUP * g : GROUP * (g + 1)] = total.reshape(GROUP, BLOCK, total.shape[-1])

    for c in loads[8:]:
        c.wait()
    agenda = []
    for g in range(groups):
        for delay, rank, act in ((2, 0, pick), (4, 1, pass_on), (7, 2, out_of_hidden), (5, 3, into_hidden)):
            agenda.append((2 * g + delay, rank, g, act))
    agenda.sort(key=lambda entry: entry[:3])

    def run(step):
        while agenda and (step is None or agenda[0][0] <= step):
            _, _, g, act = agenda.pop(0)
            act(g)

    for step in range(1, up + 1):
        note_up(step - 1).wait_recv()
        if step < up:
            note_up(step).start()
        if step <= down:
            note_down(step - 1).wait_recv()
            if step < down:
                note_down(step).start()
        for p in range(PIECES):
            up_copy(step - 1, p).wait_recv()
            if step < up:
                up_copy(step, p).start()
            if step <= down:
                down_copy(step - 1, p).wait_recv()
                if step < down:
                    down_copy(step, p).start()
        run(step)
    run(None)

    part_width = partial.shape[-1] // SPLIT

    def part(place, s):
        return partial[place, :, s * part_width : (s + 1) * part_width]

    def fall_copy(k, s):
        return copy_to(
            fall_out.at[k - 1, s], fall_in.at[k - 1, s],
            fall_send.at[k - 1, s], fall_recv.at[k - 1, s], moved(me, n, z=next_stop(k) - k),
        )

    def rise_copy(k, s):
        return copy_to(
            rise_out.at[k - 1, s], rise_in.at[k - 1, s],
            rise_send.at[k - 1, s], rise_recv.at[k - 1, s], moved(me, n, z=k - next_stop(k)),
        )

    mixed_groups = set()

    def need(place):
        if place // GROUP not in mixed_groups:
            mixed_groups.add(place // GROUP)
            mix(place // GROUP)

    def gathered(total, k, s, copy, buffer, farthest):
        for other in range(k + 1, farthest + 1):
            if next_stop(other) == k:
                copy(other, s).wait_recv()
                total = total + buffer[other - 1, s].astype(f32)
        return total

    def settle():
        for d in order:
            if d:
                z_copy(d).wait_send()
            for i in range(len(plane)):
                plane_copy(d, i).wait_send()
            share_copy(d, core).wait_send()
        for c in fold_copies:
            c.wait_send()
        for k in range(up):
            note_up(k).wait_send()
        for k in range(down):
            note_down(k).wait_send()
        for p in range(PIECES):
            for k in range(up):
                up_copy(k, p).wait_send()
            for k in range(down):
                down_copy(k, p).wait_send()
        for g in range(groups):
            core_copy(g, core).wait_send()
            for i in range(len(plane)):
                pick_copy(g, i).wait_send()
                ret_copy(g, i).wait_send()
            for i in range(len(tensor_steps)):
                hid_copy(g, i).wait_send()

    for t in range(up):
        k, j = up - t, down - t
        need(2 * k - 1)
        if j >= 1:
            need(2 * j)
        for s in range(SPLIT):
            fall_out[k - 1, s] = gathered(part(2 * k - 1, s), k, s, fall_copy, fall_in, up).astype(bf16)
            fall_copy(k, s).start()
            if j >= 1:
                rise_out[j - 1, s] = gathered(part(2 * j, s), j, s, rise_copy, rise_in, down).astype(bf16)
                rise_copy(j, s).start()
        if t == 0:
            for g in range(groups - 1, -1, -1):
                need(GROUP * g)
            settle()
    for s in range(SPLIT):
        cols = slice(s * part_width, (s + 1) * part_width)
        total = kept[:, cols].astype(f32) + part(0, s)
        total = gathered(total, 0, s, rise_copy, rise_in, down)
        mixed_ref[:, cols] = gathered(total, 0, s, fall_copy, fall_in, up).astype(bf16)

    for s in range(SPLIT):
        for k in range(1, up + 1):
            fall_copy(k, s).wait_send()
        for k in range(1, down + 1):
            rise_copy(k, s).wait_send()


def body(
    q_proj,
    key_projection,
    value_projection,
    segments,
    resid,
    norm_gain,
    route_ids,
    route_gates,
    w_gate,
    w_up,
    w_down,
):
    n = sizes()
    rows, width = q_proj.shape
    plane_rows = n["xh"] * rows
    reach = min(-(-REACH // plane_rows), n["z"] - 1)
    experts = n["xh"] * n["dp"]
    tensors = n["xl"] * n["core"]
    lanes = GROUP * BLOCK
    slabs = tensors * n["dp"]
    up, down = n["z"] // 2, max(n["z"] // 2 - 1, 1)
    groups = n["z"] // GROUP
    half = slabs * width // n["core"]
    out_width = n["dp"] * width
    units = w_gate.shape[1]
    n_slots = experts * SLOTS
    part_width = out_width // SPLIT
    args = (
        q_proj, key_projection, value_projection, segments.reshape(1, -1), resid, norm_gain.reshape(-1, 128),
        route_ids.T, route_gates.T, w_gate, w_up, w_down,
    )
    held = (0, 1, 2, 3, 4, 5, 6, 7, 8, 9, 10)
    buffers = [
        ((2, reach + 1, plane_rows, HEAD_WIDTH), bf16),
        ((rows * width // HEAD_WIDTH, HEAD_WIDTH), bf16),
        ((n["z"], 2, route_ids.shape[1], lanes), f32),
        ((groups, n_slots, lanes), f32),
        ((rows, width), bf16),
        ((slabs, BLOCK, width), bf16),
        ((BLOCK, out_width), bf16),
        ((slabs * width // 128, 128), f32),
        ((n["z"], PIECES, BLOCK, half // PIECES), bf16),
        ((groups, experts, SLOTS, half), bf16),
        ((n["core"], groups, experts, SLOTS, half), bf16),
        ((groups, tensors, units, n_slots), bf16),
        ((groups, experts, SLOTS, out_width), bf16),
        ((groups, experts, SLOTS, out_width), bf16),
        ((n["z"], BLOCK, out_width), f32),
        ((up, SPLIT, BLOCK, part_width), bf16),
        ((up, SPLIT, BLOCK, part_width), bf16),
        ((down, SPLIT, BLOCK, part_width), bf16),
        ((down, SPLIT, BLOCK, part_width), bf16),
    ]
    semaphores = [
        (reach + 1,), (reach + 1, experts), (reach + 1,), (up,), (down,), (slabs,),
        (up, PIECES), (down, PIECES), (groups, experts), (groups,), (groups, tensors), (groups, experts),
        (up, SPLIT), (down, SPLIT),
    ]
    dma = pltpu.SemaphoreType.DMA
    return pl.pallas_call(
        functools.partial(layer_kernel, n),
        out_shape=jax.ShapeDtypeStruct((BLOCK, out_width), bf16),
        in_specs=[pl.BlockSpec(memory_space=pl.ANY)] * len(args),
        out_specs=pl.BlockSpec(memory_space=pltpu.VMEM),
        scratch_shapes=[pltpu.VMEM(args[i].shape, args[i].dtype) for i in held]
        + [pltpu.VMEM(*b) for b in buffers]
        + [dma((len(args),))]
        + [dma(shape) for shape in semaphores for _ in range(2)],
        compiler_params=pltpu.CompilerParams(
            collective_id=0, has_side_effects=True, vmem_limit_bytes=56 * 1024 * 1024
        ),
        name="layer",
    )(*args)


def solution(mesh):
    n_cp, n_tp, n_dp = (mesh.shape[a] for a in ("cp", "tp", "dp"))
    fine = Mesh(
        mesh.devices.reshape(n_cp // 2, 2, n_tp // 2, 2, n_dp), ("z", "xh", "xl", "core", "dp")
    )
    cp, tp = ("z", "xh"), ("xl", "core")
    placed = (
        P(cp, tp + ("dp",)),
        P(cp, None),
        P(cp, None),
        P(),
        P(cp, tp + ("dp",)),
        P(),
        P(cp + ("dp",), None),
        P(cp + ("dp",), None),
        P(cp + ("dp",), tp, None),
        P(cp + ("dp",), tp, None),
        P(cp + ("dp",), None, tp),
    )
    return jax.shard_map(
        body, mesh=fine, in_specs=placed, out_specs=P(cp + ("dp",), tp), check_vma=False
    )
```

```python
import functools

import jax
import jax.numpy as jnp
from jax import lax
from jax.experimental import pallas as pl
from jax.experimental.pallas import tpu as pltpu
from jax.sharding import Mesh, PartitionSpec as P

HEAD_WIDTH = 128
CAP = 4
REACH = 2048
BLOCK = 32
GROUP = 4
HALF = GROUP // 2
SLOTS = GROUP * CAP
SPLIT = 4
PIECES = 4
PASS_LAG = 3
LAG_CORE, LAG_USE = 5, 2

epsilon = 1e-06
masked_score = -1e30
bf16, f32 = jnp.bfloat16, jnp.float32
MESH = pl.DeviceIdType.MESH


def sizes():
    return {a: lax.axis_size(a) for a in ("z", "xh", "xl", "core", "dp")}


def places():
    return {a: lax.axis_index(a) for a in ("z", "xh", "xl", "core", "dp")}


def moved(me, n, **steps):
    return {a: lax.rem(me[a] + n[a] + s, n[a]) for a, s in steps.items()}


def shifts(n, axes):
    found = [{}]
    for a in axes:
        found = [{**f, a: s} for f in found for s in range(n[a])]
    return found[1:]


def copy_to(src, dst, send, recv, device):
    return pltpu.make_async_remote_copy(
        src_ref=src, dst_ref=dst, send_sem=send, recv_sem=recv, device_id=device, device_id_type=MESH
    )


def greet(me, n, steps):
    barrier = pltpu.get_barrier_semaphore()
    for s in steps:
        pl.semaphore_signal(barrier, inc=1, device_id=moved(me, n, **s), device_id_type=MESH)
    return lambda: pl.semaphore_wait(barrier, len(steps))


def stops(far, late, meet):
    if late <= 1:
        return {k: k - 1 for k in range(1, far + 1)}
    found = {k: k - 1 for k in range(1, far + 1)}
    found[late] = meet
    found[meet] = 0
    return found


def up_place(k):
    return 2 * k - 1 if k else 0


def layer_kernel(
    n, q_hbm, k_hbm, v_hbm, seg_hbm, resid_hbm, gain_hbm, ids_hbm, gates_hbm, w_gate_hbm, w_up_hbm, w_down_hbm,
    mixed_ref,
    q_ref, k_ref, v_ref, seg_ref, resid_ref, gain_ref, ids_ref, gates_ref, w_gate, w_up, w_down,
    kv, queries, notes, stage, fold, kept, wide_gain,
    tokens, picked, arrived, hidden, produced, returned, partial, fall_out, fall_in, rise_out, rise_in,
    in_sem, z_send, z_recv, plane_send, plane_recv, share_send, share_recv,
    note_up_send, note_up_recv, note_down_send, note_down_recv, fold_send, fold_recv,
    up_send, up_recv, down_send, down_recv, pick_send, pick_recv, core_send, core_recv,
    hid_send, hid_recv, ret_send, ret_recv, fall_send, fall_recv, rise_send, rise_recv,
):
    me = places()
    rows = q_ref.shape[0]
    heads = q_ref.shape[1] // HEAD_WIDTH
    plane_rows = n["xh"] * rows
    reach = min(-(-REACH // plane_rows), n["z"] - 1)
    up, down = n["z"] // 2, n["z"] // 2 - 1
    groups = n["z"] // GROUP
    plane = shifts(n, ("xh", "dp"))
    group = shifts(n, ("xl", "core", "dp"))
    tensor_steps = shifts(n, ("xl", "core"))
    near = -(-reach // 2)
    line = [{"z": s} for s in range(1, n["z"]) if min(s, n["z"] - s) <= near]
    core = me["core"]
    tensor = me["xl"] * n["core"] + core
    mine = me["xh"] * n["dp"] + me["dp"]
    experts = n["xh"] * n["dp"]

    crossed = [{**p, "xl": n["xl"] // 2 if p["xh"] else 0} for p in plane]
    met = greet(
        me, n,
        line + plane + [g for g in group if g["xl"] or g["core"]] + [p for p in crossed if p["xl"]],
    )
    pairs = (
        (k_hbm, k_ref), (v_hbm, v_ref), (ids_hbm, ids_ref), (gates_hbm, gates_ref), (q_hbm, q_ref),
        (seg_hbm, seg_ref), (resid_hbm, resid_ref), (gain_hbm, gain_ref),
        (w_gate_hbm, w_gate), (w_up_hbm, w_up), (w_down_hbm, w_down),
    )
    loads = [pltpu.make_async_copy(a, b, in_sem.at[i]) for i, (a, b) in enumerate(pairs)]
    for c in loads:
        c.start()
    met()

    quarter = rows // n["dp"]
    start = pl.multiple_of(me["xh"] * rows + me["dp"] * quarter, quarter)
    here = pl.ds(start, quarter)
    head = pl.ds(pl.multiple_of(me["xl"] * HEAD_WIDTH, HEAD_WIDTH), HEAD_WIDTH)
    own = pl.ds(pl.multiple_of(me["dp"] * quarter, quarter), quarter)
    loads[0].wait()
    loads[1].wait()
    kv[core, 0, here, :] = jnp.where(core == 0, k_ref[own, head], v_ref[own, head])

    def z_copy(d):
        first = 0 if d <= near else near
        return copy_to(
            kv.at[core, first, here], kv.at[core, d, here],
            z_send.at[d], z_recv.at[d], moved(me, n, z=d - first),
        )

    def plane_copy(d, i):
        return copy_to(
            kv.at[core, d, here], kv.at[core, d, here],
            plane_send.at[d, i], plane_recv.at[d, i], moved(me, n, **plane[i]),
        )

    def share_copy(d, which):
        return copy_to(
            kv.at[which, d], kv.at[which, d], share_send.at[d], share_recv.at[d], moved(me, n, core=1)
        )

    order = [0, near] + [d for d in range(1, reach + 1) if d != near]
    for d in order[1 : near + 1]:
        z_copy(d).start()
    for i in range(len(plane)):
        plane_copy(0, i).start()

    lanes = notes.shape[-1]
    token = lax.broadcasted_iota(jnp.int32, (BLOCK, lanes), 0)
    lane = lax.broadcasted_iota(jnp.int32, (BLOCK, lanes), 1)
    spread = jnp.where(lax.rem(lane, BLOCK) == token, 1.0, 0.0)
    over = (((0,), (0,)), ((), ()))
    exact = dict(preferred_element_type=f32, precision=lax.Precision.HIGHEST)
    loads[2].wait()
    loads[3].wait()
    notes[0, 0] = jnp.dot(ids_ref[...].astype(f32), spread, **exact)
    notes[0, 1] = jnp.dot(gates_ref[...], spread, **exact)

    def note_up(k):
        return copy_to(
            notes.at[up_place(k)], notes.at[up_place(k + 1)],
            note_up_send.at[k], note_up_recv.at[k], moved(me, n, z=1),
        )

    def note_down(k):
        return copy_to(
            notes.at[2 * k], notes.at[2 * k + 2],
            note_down_send.at[k], note_down_recv.at[k], moved(me, n, z=-1),
        )

    note_up(0).start()
    note_down(0).start()

    for c in loads[4:8]:
        c.wait()
    wide_gain[...] = gain_ref[...].astype(f32)
    for h in range(heads):
        queries[h * rows : (h + 1) * rows] = q_ref[:, h * HEAD_WIDTH : (h + 1) * HEAD_WIDTH]
    all_rows = heads * rows
    context = me["z"] * n["xh"] + me["xh"]
    first_row = pl.multiple_of(context * rows, rows)
    seg_here = seg_ref[:, pl.ds(first_row, rows)].astype(f32)
    r = lax.broadcasted_iota(jnp.int32, (all_rows, rows), 0)
    c = lax.broadcasted_iota(jnp.int32, (all_rows, rows), 1)
    seg_rows = jnp.sum(jnp.where(lax.rem(r, rows) == c, seg_here, 0.0), 1, keepdims=True)
    q_position = first_row + lax.rem(
        lax.broadcasted_iota(jnp.int32, (all_rows, plane_rows), 0), rows
    )
    k_offset = lax.broadcasted_iota(jnp.int32, (all_rows, plane_rows), 1)
    state = None
    for t in range(len(order) + LAG_CORE + LAG_USE):
        if 1 <= t < len(order):
            z_copy(order[t]).wait_recv()
            if order[t] == near:
                for d in range(near + 1, reach + 1):
                    z_copy(d).start()
            for i in range(len(plane)):
                plane_copy(order[t], i).start()
        if 0 <= t - LAG_CORE < len(order):
            for i in range(len(plane)):
                plane_copy(order[t - LAG_CORE], i).wait_recv()
            share_copy(order[t - LAG_CORE], core).start()
        if t < LAG_CORE + LAG_USE:
            continue
        d = order[t - LAG_CORE - LAG_USE]
        share_copy(d, 1 - core).wait_recv()
        first_key = pl.multiple_of(lax.rem(me["z"] + n["z"] - d, n["z"]) * plane_rows, plane_rows)
        scores = (
            lax.dot_general(
                queries[...], kv[0, d], (((1,), (1,)), ((), ())), preferred_element_type=f32
            )
            * HEAD_WIDTH ** (-0.5)
        )
        seg_keys = seg_ref[:, pl.ds(first_key, plane_rows)].astype(f32)
        allowed = (first_key + k_offset <= q_position) & (seg_keys == seg_rows)
        scores = jnp.where(allowed, scores, masked_score)
        top = jnp.max(scores, 1, keepdims=True)
        if state is None:
            weights = jnp.exp(scores - top)
            total = jnp.sum(weights, 1, keepdims=True)
            acc = jnp.dot(weights.astype(bf16), kv[1, d], preferred_element_type=f32)
        else:
            old_top, old_total, old_acc = state
            top = jnp.maximum(old_top, top)
            weights = jnp.exp(scores - top)
            fade = jnp.exp(old_top - top)
            total = old_total * fade + jnp.sum(weights, 1, keepdims=True)
            acc = old_acc * fade + jnp.dot(
                weights.astype(bf16), kv[1, d], preferred_element_type=f32
            )
        state = (top, total, acc)
    attended = state[2] / state[1]
    for h in range(heads):
        cols = slice(h * HEAD_WIDTH, (h + 1) * HEAD_WIDTH)
        stage[:, cols] = (
            resid_ref[:, cols].astype(f32) + attended[h * rows : (h + 1) * rows]
        ).astype(bf16)

    slab = tensor * n["dp"] + me["dp"]

    def rows_for(y):
        return pl.ds(pl.multiple_of(y * quarter, quarter), quarter)

    fold_copies = []
    for i, g in enumerate(group):
        target = moved(me, n, **g)
        fold_copies.append(
            copy_to(
                stage.at[rows_for(target["dp"])], fold.at[slab],
                fold_send.at[i], fold_recv.at[i], target,
            )
        )
        fold_copies[-1].start()
    fold[slab] = stage[rows_for(me["dp"]), :]
    for f in fold_copies:
        f.wait_recv()
    slabs = fold.shape[0]
    width = stage.shape[1]
    squares = jnp.zeros((quarter, width), f32)
    for s in range(slabs):
        v = fold[s].astype(f32)
        squares += v * v
    squares = jnp.sum(squares, 1, keepdims=True)
    inverse = lax.rsqrt(squares / (slabs * width) + epsilon)
    per_core = slabs // n["core"]
    piece_width = tokens.shape[3]

    def up_copy(k, p):
        return copy_to(
            tokens.at[up_place(k), p], tokens.at[up_place(k + 1), p],
            up_send.at[k, p], up_recv.at[k, p], moved(me, n, z=1),
        )

    def down_copy(k, p):
        return copy_to(
            tokens.at[2 * k, p], tokens.at[2 * k + 2, p],
            down_send.at[k, p], down_recv.at[k, p], moved(me, n, z=-1),
        )

    for i in range(per_core):
        s = core * per_core + i
        lines = [wide_gain[pl.ds(s * (width // 128) + r, 1), :] for r in range(width // 128)]
        gain = jnp.concatenate(lines, 1)
        p, q = divmod(i * width, piece_width)
        tokens[0, p, :, q : q + width] = (fold[s].astype(f32) * inverse * gain).astype(bf16)
        if q + width == piece_width:
            up_copy(0, p).start()
            down_copy(0, p).start()
    for i in range(n["dp"]):
        kept[:, i * width : (i + 1) * width] = fold[tensor * n["dp"] + i]

    def pick_copy(g, i):
        to = moved(me, n, **crossed[i])
        return copy_to(
            picked.at[g, to["xh"] * n["dp"] + to["dp"]], arrived.at[core, g, mine],
            pick_send.at[g, i], pick_recv.at[g, i], to,
        )

    def core_copy(g, half):
        return copy_to(
            arrived.at[half, g], arrived.at[half, g],
            core_send.at[g], core_recv.at[g], moved(me, n, core=1),
        )

    def hid_copy(g, i):
        return copy_to(
            hidden.at[g, tensor], hidden.at[g, tensor],
            hid_send.at[g, i], hid_recv.at[g, i], moved(me, n, **tensor_steps[i]),
        )

    def ret_copy(g, i):
        to = moved(me, n, **{a: -s for a, s in plane[i].items()})
        return copy_to(
            produced.at[g, to["xh"] * n["dp"] + to["dp"]], returned.at[g, mine],
            ret_send.at[g, i], ret_recv.at[g, i], to,
        )

    def slots_of(first, count):
        row = lax.broadcasted_iota(jnp.int32, (lanes, lanes), 0)
        column = lax.broadcasted_iota(jnp.int32, (lanes, lanes), 1)
        before = (row < column) & (row // BLOCK == column // BLOCK)
        lane = lax.broadcasted_iota(jnp.int32, notes.shape[2:], 1)
        ids, gates = notes[first, 0], notes[first, 1]
        for j in range(1, count):
            inside = lane // BLOCK == j
            ids = jnp.where(inside, notes[first + j, 0], ids)
            gates = jnp.where(inside, notes[first + j, 1], gates)
        expert = me["z"] * experts + lax.broadcasted_iota(jnp.int32, (experts, lanes), 0)
        expert = expert.astype(f32)
        named = jnp.zeros((experts, lanes), f32)
        weight = jnp.zeros((experts, lanes), f32)
        for j in range(ids.shape[0]):
            equal = jnp.abs(expert - ids[j : j + 1, :]) < 0.5
            named += jnp.where(equal, 1.0, 0.0)
            weight += jnp.where(equal, gates[j : j + 1, :], 0.0)
        rank = jnp.dot(
            named.astype(bf16), jnp.where(before, 1.0, 0.0).astype(bf16), preferred_element_type=f32
        )
        rank = jnp.where(named > 0.5, rank, 2.0 * CAP)
        shape = (experts, count * CAP, lanes)
        slot = lax.broadcasted_iota(jnp.int32, shape, 1)
        token = lax.broadcasted_iota(jnp.int32, shape, 2)
        held = (jnp.broadcast_to(rank[:, None, :], shape) == lax.rem(slot, CAP).astype(f32)) & (
            token // BLOCK == slot // CAP
        )
        weight = jnp.where(held, jnp.broadcast_to(weight[:, None, :], shape), 0.0)
        flat = (experts * count * CAP, lanes)
        return jnp.where(held, 1.0, 0.0).reshape(flat), weight.reshape(flat)

    def pick(q):
        chosen, _ = slots_of(HALF * q, HALF)
        chosen = chosen[:, : HALF * BLOCK].astype(bf16)

        def taken(p):
            block = tokens[HALF * q : HALF * (q + 1), p].reshape(HALF * BLOCK, piece_width)
            out = jnp.dot(chosen, block, preferred_element_type=f32)
            return out.reshape(experts, HALF * CAP, piece_width)

        for p in range(PIECES // 2):
            both = jnp.concatenate([taken(p), taken(p + PIECES // 2)], 1)
            picked[q, :, :, p * piece_width : (p + 1) * piece_width] = both.astype(bf16)
        for i in range(len(plane)):
            pick_copy(q, i).start()
        arrived[core, q, mine] = picked[q, mine]

    def pass_on(g):
        for i in range(len(plane)):
            pick_copy(g, i).wait_recv()
        core_copy(g, core).start()

    contract = (((1,), (1,)), ((), ()))
    n_slots = experts * SLOTS

    def into_hidden(g):
        parts = range(HALF * g, HALF * (g + 1))
        for q in parts:
            core_copy(q, 1 - core).wait_recv()
        gate_val = up_val = None
        span = arrived.shape[-1]
        for h in range(n["core"]):
            values = [arrived[h, q].astype(f32) for q in parts]
            for r in range(2):
                rows_here = slice(r * HALF * CAP, (r + 1) * HALF * CAP)
                x = jnp.concatenate(
                    [v[:, rows_here].reshape(experts * HALF * CAP, span) for v in values], 0
                ).astype(bf16)
                cols = slice((2 * h + r) * span, (2 * h + r + 1) * span)
                a = lax.dot_general(w_gate[0, :, cols], x, contract, preferred_element_type=f32)
                b = lax.dot_general(w_up[0, :, cols], x, contract, preferred_element_type=f32)
                gate_val = a if gate_val is None else gate_val + a
                up_val = b if up_val is None else up_val + b
        hidden[g, tensor] = (gate_val / (1.0 + jnp.exp(-gate_val)) * up_val).astype(bf16)
        for i in range(len(tensor_steps)):
            hid_copy(g, i).start()

    def out_of_hidden(g):
        for i in range(len(tensor_steps)):
            hid_copy(g, i).wait_recv()
        units = hidden[g].reshape(w_down.shape[1], n_slots)
        out = lax.dot_general(units, w_down[0], over, preferred_element_type=f32)
        out = out.reshape(2, experts, HALF * CAP, out.shape[-1])
        produced[g] = jnp.concatenate([out[0], out[1]], 1).astype(bf16)
        for i in range(len(plane)):
            ret_copy(g, i).start()
        returned[g, mine] = produced[g, mine]

    def mix(g):
        _, weight = slots_of(GROUP * g, GROUP)
        for i in range(len(plane)):
            ret_copy(g, i).wait_recv()
        high = weight.astype(bf16)
        low = (weight - high.astype(f32)).astype(bf16)
        back = returned[g].reshape(n_slots, returned.shape[-1])
        total = lax.dot_general(high, back, over, preferred_element_type=f32)
        total += lax.dot_general(low, back, over, preferred_element_type=f32)
        partial[GROUP * g : GROUP * (g + 1)] = total.reshape(GROUP, BLOCK, total.shape[-1])

    for c in loads[8:]:
        c.wait()
    agenda = []
    for g in range(groups):
        for delay, rank, act in ((6, 2, out_of_hidden), (5, 3, into_hidden)):
            if act is into_hidden or g < groups - 1:
                agenda.append((2 * g + delay, rank, g, act))
        for q in range(2 * g, 2 * g + 2):
            agenda += [(q + 1, 0, q, pick), (q + PASS_LAG, 1, q, pass_on)]
    agenda.sort(key=lambda entry: entry[:3])

    def run(step):
        while agenda and (step is None or agenda[0][0] <= step):
            _, _, g, act = agenda.pop(0)
            act(g)

    for step in range(1, up + 1):
        note_up(step - 1).wait_recv()
        if step < up:
            note_up(step).start()
        if step <= down:
            note_down(step - 1).wait_recv()
            if step < down:
                note_down(step).start()
        for p in range(PIECES):
            up_copy(step - 1, p).wait_recv()
            if step < up:
                up_copy(step, p).start()
            if step <= down:
                down_copy(step - 1, p).wait_recv()
                if step < down:
                    down_copy(step, p).start()
        run(step)
    run(None)
    for g in range(groups - 2):
        mix(g)
    out_of_hidden(groups - 1)
    if groups > 1:
        mix(groups - 2)

    part_width = partial.shape[-1] // SPLIT
    last = GROUP * (groups - 1)
    fall_late, rise_late = last // 2 + 1, max(last // 2, 1)
    if groups == 1:
        fall_late = rise_late = 1
    fall_meet, rise_meet = min(near, fall_late) - 1, min(near, rise_late) - 1
    fall_stops, rise_stops = stops(up, fall_late, fall_meet), stops(down, rise_late, rise_meet)

    def part(place, s):
        return partial[place, :, s * part_width : (s + 1) * part_width]

    def fall_copy(k, s):
        return copy_to(
            fall_out.at[k - 1, s], fall_in.at[k - 1, s],
            fall_send.at[k - 1, s], fall_recv.at[k - 1, s], moved(me, n, z=fall_stops[k] - k),
        )

    def rise_copy(k, s):
        return copy_to(
            rise_out.at[k - 1, s], rise_in.at[k - 1, s],
            rise_send.at[k - 1, s], rise_recv.at[k - 1, s], moved(me, n, z=k - rise_stops[k]),
        )

    def settle():
        for d in order:
            if d:
                z_copy(d).wait_send()
            for i in range(len(plane)):
                plane_copy(d, i).wait_send()
            share_copy(d, core).wait_send()
        for c in fold_copies:
            c.wait_send()
        for k in range(up):
            note_up(k).wait_send()
        for k in range(down):
            note_down(k).wait_send()
        for p in range(PIECES):
            for k in range(up):
                up_copy(k, p).wait_send()
            for k in range(down):
                down_copy(k, p).wait_send()
        for q in range(2 * groups):
            core_copy(q, core).wait_send()
            for i in range(len(plane)):
                pick_copy(q, i).wait_send()
        for g in range(groups):
            for i in range(len(plane)):
                ret_copy(g, i).wait_send()
            for i in range(len(tensor_steps)):
                hid_copy(g, i).wait_send()

    def gathered(total, k, s, copy, buffer, where):
        for other in sorted(where):
            if where[other] == k:
                copy(other, s).wait_recv()
                total = total + buffer[other - 1, s].astype(f32)
        return total

    def fall(k):
        for s in range(SPLIT):
            total = gathered(part(2 * k - 1, s), k, s, fall_copy, fall_in, fall_stops)
            fall_out[k - 1, s] = total.astype(bf16)
            fall_copy(k, s).start()

    def rise(k):
        for s in range(SPLIT):
            total = gathered(part(2 * k, s), k, s, rise_copy, rise_in, rise_stops)
            rise_out[k - 1, s] = total.astype(bf16)
            rise_copy(k, s).start()

    def in_turn(*lines):
        for i in range(max(len(ks) for _, ks in lines)):
            for act, ks in lines:
                if i < len(ks):
                    act(ks[i])

    def back_from(high, low):
        return list(range(high, low, -1))

    in_turn(
        (fall, back_from(fall_late - 1, fall_meet)),
        (rise, back_from(rise_late - 1, rise_meet)),
        (fall, back_from(fall_meet - 1, 0)),
        (rise, back_from(rise_meet - 1, 0)),
    )
    mix(groups - 1)
    fall_last = back_from(up, fall_late - 1) + [fall_meet] * (fall_meet > 0)
    rise_last = back_from(down, rise_late - 1) + [rise_meet] * (rise_meet > 0)
    in_turn((fall, fall_last[:1]), (rise, rise_last[:1]))
    settle()
    in_turn((fall, fall_last[1:]), (rise, rise_last[1:]))
    for s in range(SPLIT):
        cols = slice(s * part_width, (s + 1) * part_width)
        total = kept[:, cols].astype(f32) + part(0, s)
        total = gathered(total, 0, s, rise_copy, rise_in, rise_stops)
        mixed_ref[:, cols] = gathered(total, 0, s, fall_copy, fall_in, fall_stops).astype(bf16)

    for s in range(SPLIT):
        for k in range(1, up + 1):
            fall_copy(k, s).wait_send()
        for k in range(1, down + 1):
            rise_copy(k, s).wait_send()


def body(
    q_proj,
    key_projection,
    value_projection,
    segments,
    resid,
    norm_gain,
    route_ids,
    route_gates,
    w_gate,
    w_up,
    w_down,
):
    n = sizes()
    rows, width = q_proj.shape
    plane_rows = n["xh"] * rows
    reach = min(-(-REACH // plane_rows), n["z"] - 1)
    experts = n["xh"] * n["dp"]
    tensors = n["xl"] * n["core"]
    lanes = GROUP * BLOCK
    slabs = tensors * n["dp"]
    up, down = n["z"] // 2, max(n["z"] // 2 - 1, 1)
    groups = n["z"] // GROUP
    half = slabs * width // n["core"]
    out_width = n["dp"] * width
    units = w_gate.shape[1]
    n_slots = experts * SLOTS
    part_width = out_width // SPLIT
    args = (
        q_proj, key_projection, value_projection, segments.reshape(1, -1), resid, norm_gain.reshape(-1, 128),
        route_ids.T, route_gates.T, w_gate, w_up, w_down,
    )
    held = (0, 1, 2, 3, 4, 5, 6, 7, 8, 9, 10)
    buffers = [
        ((2, reach + 1, plane_rows, HEAD_WIDTH), bf16),
        ((rows * width // HEAD_WIDTH, HEAD_WIDTH), bf16),
        ((n["z"], 2, route_ids.shape[1], lanes), f32),
        ((rows, width), bf16),
        ((slabs, BLOCK, width), bf16),
        ((BLOCK, out_width), bf16),
        ((slabs * width // 128, 128), f32),
        ((n["z"], PIECES, BLOCK, half // PIECES), bf16),
        ((2 * groups, experts, SLOTS, half // 2), bf16),
        ((n["core"], 2 * groups, experts, SLOTS, half // 2), bf16),
        ((groups, tensors, units, n_slots), bf16),
        ((groups, experts, SLOTS, out_width), bf16),
        ((groups, experts, SLOTS, out_width), bf16),
        ((n["z"], BLOCK, out_width), f32),
        ((up, SPLIT, BLOCK, part_width), bf16),
        ((up, SPLIT, BLOCK, part_width), bf16),
        ((down, SPLIT, BLOCK, part_width), bf16),
        ((down, SPLIT, BLOCK, part_width), bf16),
    ]
    semaphores = [
        (reach + 1,), (reach + 1, experts), (reach + 1,), (up,), (down,), (slabs,),
        (up, PIECES), (down, PIECES), (2 * groups, experts), (2 * groups,), (groups, tensors), (groups, experts),
        (up, SPLIT), (down, SPLIT),
    ]
    dma = pltpu.SemaphoreType.DMA
    return pl.pallas_call(
        functools.partial(layer_kernel, n),
        out_shape=jax.ShapeDtypeStruct((BLOCK, out_width), bf16),
        in_specs=[pl.BlockSpec(memory_space=pl.ANY)] * len(args),
        out_specs=pl.BlockSpec(memory_space=pltpu.VMEM),
        scratch_shapes=[pltpu.VMEM(args[i].shape, args[i].dtype) for i in held]
        + [pltpu.VMEM(*b) for b in buffers]
        + [dma((len(args),))]
        + [dma(shape) for shape in semaphores for _ in range(2)],
        compiler_params=pltpu.CompilerParams(
            collective_id=0, has_side_effects=True, vmem_limit_bytes=56 * 1024 * 1024
        ),
        name="layer",
    )(*args)


def solution(mesh):
    n_cp, n_tp, n_dp = (mesh.shape[a] for a in ("cp", "tp", "dp"))
    fine = Mesh(
        mesh.devices.reshape(n_cp // 2, 2, n_tp // 2, 2, n_dp), ("z", "xh", "xl", "core", "dp")
    )
    cp, tp = ("z", "xh"), ("xl", "core")
    placed = (
        P(cp, tp + ("dp",)),
        P(cp, None),
        P(cp, None),
        P(),
        P(cp, tp + ("dp",)),
        P(),
        P(cp + ("dp",), None),
        P(cp + ("dp",), None),
        P(cp + ("dp",), tp, None),
        P(cp + ("dp",), tp, None),
        P(cp + ("dp",), None, tp),
    )
    return jax.shard_map(
        body, mesh=fine, in_specs=placed, out_specs=P(cp + ("dp",), tp), check_vma=False
    )
```

```python
import functools

import jax
import jax.numpy as jnp
from jax import lax
from jax.experimental import pallas as pl
from jax.experimental.pallas import tpu as pltpu
from jax.sharding import Mesh, PartitionSpec as P

HEAD_WIDTH = 128
CAP = 4
REACH = 2048
BLOCK = 32
GROUP = 4
HALF = GROUP // 2
SLOTS = GROUP * CAP
SPLIT = 4
PIECES = 4
PASS_LAG = 3
LAG_CORE, LAG_USE = 5, 2

epsilon = 1e-06
masked_score = -1e30
bf16, f32 = jnp.bfloat16, jnp.float32
MESH = pl.DeviceIdType.MESH


def sizes():
    return {a: lax.axis_size(a) for a in ("z", "xh", "xl", "core", "dp")}


def places():
    return {a: lax.axis_index(a) for a in ("z", "xh", "xl", "core", "dp")}


def moved(me, n, **steps):
    return {a: lax.rem(me[a] + n[a] + s, n[a]) for a, s in steps.items()}


def shifts(n, axes):
    found = [{}]
    for a in axes:
        found = [{**f, a: s} for f in found for s in range(n[a])]
    links = {"xh": 2, "xl": 1, "dp": 1, "core": 0}
    return sorted(found[1:], key=lambda f: -sum(links[a] * min(s, n[a] - s) for a, s in f.items()))


def copy_to(src, dst, send, recv, device):
    return pltpu.make_async_remote_copy(
        src_ref=src, dst_ref=dst, send_sem=send, recv_sem=recv, device_id=device, device_id_type=MESH
    )


def greet(me, n, steps):
    barrier = pltpu.get_barrier_semaphore()
    for s in steps:
        pl.semaphore_signal(barrier, inc=1, device_id=moved(me, n, **s), device_id_type=MESH)
    return lambda: pl.semaphore_wait(barrier, len(steps))


def stops(far, late, meet):
    if late <= 1:
        return {k: k - 1 for k in range(1, far + 1)}
    found = {k: k - 1 for k in range(1, far + 1)}
    found[late] = meet
    found[meet] = 0
    return found


def up_place(k):
    return 2 * k - 1 if k else 0


def layer_kernel(
    n, q_hbm, k_hbm, v_hbm, seg_hbm, resid_hbm, gain_hbm, ids_hbm, gates_hbm, w_gate_hbm, w_up_hbm, w_down_hbm,
    mixed_ref,
    q_ref, k_ref, v_ref, seg_ref, resid_ref, gain_ref, ids_ref, gates_ref, w_gate, w_up, w_down,
    kv, queries, notes, stage, fold, kept, wide_gain,
    tokens, picked, arrived, hidden, produced, returned, partial, fall_out, fall_in, rise_out, rise_in,
    in_sem, z_send, z_recv, plane_send, plane_recv, share_send, share_recv,
    note_up_send, note_up_recv, note_down_send, note_down_recv, fold_send, fold_recv,
    up_send, up_recv, down_send, down_recv, pick_send, pick_recv, core_send, core_recv,
    hid_send, hid_recv, ret_send, ret_recv, fall_send, fall_recv, rise_send, rise_recv,
):
    me = places()
    rows = q_ref.shape[0]
    heads = q_ref.shape[1] // HEAD_WIDTH
    plane_rows = n["xh"] * rows
    reach = min(-(-REACH // plane_rows), n["z"] - 1)
    up, down = n["z"] // 2, n["z"] // 2 - 1
    groups = n["z"] // GROUP
    plane = shifts(n, ("xh", "dp"))
    group = shifts(n, ("xl", "core", "dp"))
    tensor_steps = shifts(n, ("xl", "core"))
    near = -(-reach // 2)
    line = [{"z": s} for s in range(1, n["z"]) if min(s, n["z"] - s) <= near]
    core = me["core"]
    tensor = me["xl"] * n["core"] + core
    mine = me["xh"] * n["dp"] + me["dp"]
    experts = n["xh"] * n["dp"]

    crossed = [{**p, "xl": n["xl"] // 2 if p["xh"] else 0} for p in plane]
    met = greet(
        me, n,
        line + plane + [g for g in group if g["xl"] or g["core"]] + [p for p in crossed if p["xl"]],
    )
    pairs = (
        (k_hbm, k_ref), (v_hbm, v_ref), (ids_hbm, ids_ref), (gates_hbm, gates_ref), (q_hbm, q_ref),
        (seg_hbm, seg_ref), (resid_hbm, resid_ref), (gain_hbm, gain_ref),
        (w_gate_hbm, w_gate), (w_up_hbm, w_up), (w_down_hbm, w_down),
    )
    loads = [pltpu.make_async_copy(a, b, in_sem.at[i]) for i, (a, b) in enumerate(pairs)]
    for c in loads:
        c.start()
    met()

    quarter = rows // n["dp"]
    start = pl.multiple_of(me["xh"] * rows + me["dp"] * quarter, quarter)
    here = pl.ds(start, quarter)
    head = pl.ds(pl.multiple_of(me["xl"] * HEAD_WIDTH, HEAD_WIDTH), HEAD_WIDTH)
    own = pl.ds(pl.multiple_of(me["dp"] * quarter, quarter), quarter)
    loads[0].wait()
    loads[1].wait()
    kv[core, 0, here, :] = jnp.where(core == 0, k_ref[own, head], v_ref[own, head])

    def z_copy(d):
        first = 0 if d <= near else near
        return copy_to(
            kv.at[core, first, here], kv.at[core, d, here],
            z_send.at[d], z_recv.at[d], moved(me, n, z=d - first),
        )

    def plane_copy(d, i):
        return copy_to(
            kv.at[core, d, here], kv.at[core, d, here],
            plane_send.at[d, i], plane_recv.at[d, i], moved(me, n, **plane[i]),
        )

    def share_copy(d, which):
        return copy_to(
            kv.at[which, d], kv.at[which, d], share_send.at[d], share_recv.at[d], moved(me, n, core=1)
        )

    order = [0, near] + [d for d in range(1, reach + 1) if d != near]
    for d in order[1 : near + 1]:
        z_copy(d).start()
    for i in range(len(plane)):
        plane_copy(0, i).start()

    lanes = notes.shape[-1]
    token = lax.broadcasted_iota(jnp.int32, (BLOCK, lanes), 0)
    lane = lax.broadcasted_iota(jnp.int32, (BLOCK, lanes), 1)
    spread = jnp.where(lax.rem(lane, BLOCK) == token, 1.0, 0.0)
    over = (((0,), (0,)), ((), ()))
    exact = dict(preferred_element_type=f32, precision=lax.Precision.HIGHEST)
    loads[2].wait()
    loads[3].wait()
    notes[0, 0] = jnp.dot(ids_ref[...].astype(f32), spread, **exact)
    notes[0, 1] = jnp.dot(gates_ref[...], spread, **exact)

    def note_up(k):
        return copy_to(
            notes.at[up_place(k)], notes.at[up_place(k + 1)],
            note_up_send.at[k], note_up_recv.at[k], moved(me, n, z=1),
        )

    def note_down(k):
        return copy_to(
            notes.at[2 * k], notes.at[2 * k + 2],
            note_down_send.at[k], note_down_recv.at[k], moved(me, n, z=-1),
        )

    note_up(0).start()
    note_down(0).start()

    for c in loads[4:8]:
        c.wait()
    wide_gain[...] = gain_ref[...].astype(f32)
    for h in range(heads):
        queries[h * rows : (h + 1) * rows] = q_ref[:, h * HEAD_WIDTH : (h + 1) * HEAD_WIDTH]
    all_rows = heads * rows
    context = me["z"] * n["xh"] + me["xh"]
    first_row = pl.multiple_of(context * rows, rows)
    seg_here = seg_ref[:, pl.ds(first_row, rows)].astype(f32)
    r = lax.broadcasted_iota(jnp.int32, (all_rows, rows), 0)
    c = lax.broadcasted_iota(jnp.int32, (all_rows, rows), 1)
    seg_rows = jnp.sum(jnp.where(lax.rem(r, rows) == c, seg_here, 0.0), 1, keepdims=True)
    q_position = first_row + lax.rem(
        lax.broadcasted_iota(jnp.int32, (all_rows, plane_rows), 0), rows
    )
    k_offset = lax.broadcasted_iota(jnp.int32, (all_rows, plane_rows), 1)
    state = None
    for t in range(len(order) + LAG_CORE + LAG_USE):
        if 1 <= t < len(order):
            z_copy(order[t]).wait_recv()
            if order[t] == near:
                for d in range(near + 1, reach + 1):
                    z_copy(d).start()
            for i in range(len(plane)):
                plane_copy(order[t], i).start()
        if 0 <= t - LAG_CORE < len(order):
            for i in range(len(plane)):
                plane_copy(order[t - LAG_CORE], i).wait_recv()
            share_copy(order[t - LAG_CORE], core).start()
        if t < LAG_CORE + LAG_USE:
            continue
        d = order[t - LAG_CORE - LAG_USE]
        share_copy(d, 1 - core).wait_recv()
        first_key = pl.multiple_of(lax.rem(me["z"] + n["z"] - d, n["z"]) * plane_rows, plane_rows)
        scores = (
            lax.dot_general(
                queries[...], kv[0, d], (((1,), (1,)), ((), ())), preferred_element_type=f32
            )
            * HEAD_WIDTH ** (-0.5)
        )
        seg_keys = seg_ref[:, pl.ds(first_key, plane_rows)].astype(f32)
        allowed = (first_key + k_offset <= q_position) & (seg_keys == seg_rows)
        scores = jnp.where(allowed, scores, masked_score)
        top = jnp.max(scores, 1, keepdims=True)
        if state is None:
            weights = jnp.exp(scores - top)
            total = jnp.sum(weights, 1, keepdims=True)
            acc = jnp.dot(weights.astype(bf16), kv[1, d], preferred_element_type=f32)
        else:
            old_top, old_total, old_acc = state
            top = jnp.maximum(old_top, top)
            weights = jnp.exp(scores - top)
            fade = jnp.exp(old_top - top)
            total = old_total * fade + jnp.sum(weights, 1, keepdims=True)
            acc = old_acc * fade + jnp.dot(
                weights.astype(bf16), kv[1, d], preferred_element_type=f32
            )
        state = (top, total, acc)
    attended = state[2] / state[1]
    for h in range(heads):
        cols = slice(h * HEAD_WIDTH, (h + 1) * HEAD_WIDTH)
        stage[:, cols] = (
            resid_ref[:, cols].astype(f32) + attended[h * rows : (h + 1) * rows]
        ).astype(bf16)

    slab = tensor * n["dp"] + me["dp"]

    def rows_for(y):
        return pl.ds(pl.multiple_of(y * quarter, quarter), quarter)

    fold_copies = []
    for i, g in enumerate(group):
        target = moved(me, n, **g)
        fold_copies.append(
            copy_to(
                stage.at[rows_for(target["dp"])], fold.at[slab],
                fold_send.at[i], fold_recv.at[i], target,
            )
        )
        fold_copies[-1].start()
    fold[slab] = stage[rows_for(me["dp"]), :]
    for f in fold_copies:
        f.wait_recv()
    slabs = fold.shape[0]
    width = stage.shape[1]
    squares = jnp.zeros((quarter, width), f32)
    for s in range(slabs):
        v = fold[s].astype(f32)
        squares += v * v
    squares = jnp.sum(squares, 1, keepdims=True)
    inverse = lax.rsqrt(squares / (slabs * width) + epsilon)
    per_core = slabs // n["core"]
    piece_width = tokens.shape[3]

    def up_copy(k, p):
        return copy_to(
            tokens.at[up_place(k), p], tokens.at[up_place(k + 1), p],
            up_send.at[k, p], up_recv.at[k, p], moved(me, n, z=1),
        )

    def down_copy(k, p):
        return copy_to(
            tokens.at[2 * k, p], tokens.at[2 * k + 2, p],
            down_send.at[k, p], down_recv.at[k, p], moved(me, n, z=-1),
        )

    for i in range(per_core):
        s = core * per_core + i
        lines = [wide_gain[pl.ds(s * (width // 128) + r, 1), :] for r in range(width // 128)]
        gain = jnp.concatenate(lines, 1)
        p, q = divmod(i * width, piece_width)
        tokens[0, p, :, q : q + width] = (fold[s].astype(f32) * inverse * gain).astype(bf16)
        if q + width == piece_width:
            up_copy(0, p).start()
            down_copy(0, p).start()
    for i in range(n["dp"]):
        kept[:, i * width : (i + 1) * width] = fold[tensor * n["dp"] + i]

    def pick_copy(g, i):
        to = moved(me, n, **crossed[i])
        return copy_to(
            picked.at[g, to["xh"] * n["dp"] + to["dp"]], arrived.at[core, g, mine],
            pick_send.at[g, i], pick_recv.at[g, i], to,
        )

    def core_copy(g, half):
        return copy_to(
            arrived.at[half, g], arrived.at[half, g],
            core_send.at[g], core_recv.at[g], moved(me, n, core=1),
        )

    def hid_copy(g, i):
        return copy_to(
            hidden.at[g, tensor], hidden.at[g, tensor],
            hid_send.at[g, i], hid_recv.at[g, i], moved(me, n, **tensor_steps[i]),
        )

    def ret_copy(g, i):
        to = moved(me, n, **{a: -s for a, s in plane[i].items()})
        return copy_to(
            produced.at[g, to["xh"] * n["dp"] + to["dp"]], returned.at[g, mine],
            ret_send.at[g, i], ret_recv.at[g, i], to,
        )

    def slots_of(first, count):
        row = lax.broadcasted_iota(jnp.int32, (lanes, lanes), 0)
        column = lax.broadcasted_iota(jnp.int32, (lanes, lanes), 1)
        before = (row < column) & (row // BLOCK == column // BLOCK)
        lane = lax.broadcasted_iota(jnp.int32, notes.shape[2:], 1)
        ids, gates = notes[first, 0], notes[first, 1]
        for j in range(1, count):
            inside = lane // BLOCK == j
            ids = jnp.where(inside, notes[first + j, 0], ids)
            gates = jnp.where(inside, notes[first + j, 1], gates)
        expert = me["z"] * experts + lax.broadcasted_iota(jnp.int32, (experts, lanes), 0)
        expert = expert.astype(f32)
        named = jnp.zeros((experts, lanes), f32)
        weight = jnp.zeros((experts, lanes), f32)
        for j in range(ids.shape[0]):
            equal = jnp.abs(expert - ids[j : j + 1, :]) < 0.5
            named += jnp.where(equal, 1.0, 0.0)
            weight += jnp.where(equal, gates[j : j + 1, :], 0.0)
        rank = jnp.dot(
            named.astype(bf16), jnp.where(before, 1.0, 0.0).astype(bf16), preferred_element_type=f32
        )
        rank = jnp.where(named > 0.5, rank, 2.0 * CAP)
        shape = (experts, count * CAP, lanes)
        slot = lax.broadcasted_iota(jnp.int32, shape, 1)
        token = lax.broadcasted_iota(jnp.int32, shape, 2)
        held = (jnp.broadcast_to(rank[:, None, :], shape) == lax.rem(slot, CAP).astype(f32)) & (
            token // BLOCK == slot // CAP
        )
        weight = jnp.where(held, jnp.broadcast_to(weight[:, None, :], shape), 0.0)
        flat = (experts * count * CAP, lanes)
        return jnp.where(held, 1.0, 0.0).reshape(flat), weight.reshape(flat)

    def pick(q):
        chosen, _ = slots_of(HALF * q, HALF)
        chosen = chosen[:, : HALF * BLOCK].astype(bf16)

        def taken(p):
            block = tokens[HALF * q : HALF * (q + 1), p].reshape(HALF * BLOCK, piece_width)
            out = jnp.dot(chosen, block, preferred_element_type=f32)
            return out.reshape(experts, HALF * CAP, piece_width)

        for p in range(PIECES // 2):
            both = jnp.concatenate([taken(p), taken(p + PIECES // 2)], 1)
            picked[q, :, :, p * piece_width : (p + 1) * piece_width] = both.astype(bf16)
        for i in range(len(plane)):
            pick_copy(q, i).start()
        arrived[core, q, mine] = picked[q, mine]

    def pass_on(g):
        for i in range(len(plane)):
            pick_copy(g, i).wait_recv()
        core_copy(g, core).start()

    contract = (((1,), (1,)), ((), ()))
    n_slots = experts * SLOTS

    def into_hidden(g):
        parts = range(HALF * g, HALF * (g + 1))
        for q in parts:
            core_copy(q, 1 - core).wait_recv()
        gate_val = up_val = None
        span = arrived.shape[-1]
        for h in range(n["core"]):
            values = [arrived[h, q].astype(f32) for q in parts]
            for r in range(2):
                rows_here = slice(r * HALF * CAP, (r + 1) * HALF * CAP)
                x = jnp.concatenate(
                    [v[:, rows_here].reshape(experts * HALF * CAP, span) for v in values], 0
                ).astype(bf16)
                cols = slice((2 * h + r) * span, (2 * h + r + 1) * span)
                a = lax.dot_general(w_gate[0, :, cols], x, contract, preferred_element_type=f32)
                b = lax.dot_general(w_up[0, :, cols], x, contract, preferred_element_type=f32)
                gate_val = a if gate_val is None else gate_val + a
                up_val = b if up_val is None else up_val + b
        hidden[g, tensor] = (gate_val / (1.0 + jnp.exp(-gate_val)) * up_val).astype(bf16)
        for i in range(len(tensor_steps)):
            hid_copy(g, i).start()

    def out_of_hidden(g):
        for i in range(len(tensor_steps)):
            hid_copy(g, i).wait_recv()
        units = hidden[g].reshape(w_down.shape[1], n_slots)
        out = lax.dot_general(units, w_down[0], over, preferred_element_type=f32)
        out = out.reshape(2, experts, HALF * CAP, out.shape[-1])
        produced[g] = jnp.concatenate([out[0], out[1]], 1).astype(bf16)
        for i in range(len(plane)):
            ret_copy(g, i).start()
        returned[g, mine] = produced[g, mine]

    def mix(g):
        _, weight = slots_of(GROUP * g, GROUP)
        high = weight.astype(bf16)
        low = (weight - high.astype(f32)).astype(bf16)
        for i in range(len(plane)):
            ret_copy(g, i).wait_recv()
        back = returned[g].reshape(n_slots, returned.shape[-1])
        total = lax.dot_general(high, back, over, preferred_element_type=f32)
        total += lax.dot_general(low, back, over, preferred_element_type=f32)
        partial[GROUP * g : GROUP * (g + 1)] = total.reshape(GROUP, BLOCK, total.shape[-1])

    for c in loads[8:]:
        c.wait()
    agenda = []
    for g in range(groups):
        for delay, rank, act in ((6, 2, out_of_hidden), (5, 3, into_hidden)):
            if act is into_hidden or g < groups - 1:
                agenda.append((2 * g + delay, rank, g, act))
        for q in range(2 * g, 2 * g + 2):
            agenda += [(q + 1, 0, q, pick), (q + PASS_LAG, 1, q, pass_on)]
    agenda.sort(key=lambda entry: entry[:3])

    def run(step):
        while agenda and (step is None or agenda[0][0] <= step):
            _, _, g, act = agenda.pop(0)
            act(g)

    for step in range(1, up + 1):
        note_up(step - 1).wait_recv()
        if step < up:
            note_up(step).start()
        if step <= down:
            note_down(step - 1).wait_recv()
            if step < down:
                note_down(step).start()
        for p in range(PIECES):
            up_copy(step - 1, p).wait_recv()
            if step < up:
                up_copy(step, p).start()
            if step <= down:
                down_copy(step - 1, p).wait_recv()
                if step < down:
                    down_copy(step, p).start()
        run(step)
    run(None)
    for g in range(groups - 2):
        mix(g)
    out_of_hidden(groups - 1)
    if groups > 1:
        mix(groups - 2)

    part_width = partial.shape[-1] // SPLIT
    last = GROUP * (groups - 1)
    fall_late, rise_late = last // 2 + 1, max(last // 2, 1)
    if groups == 1:
        fall_late = rise_late = 1
    fall_meet, rise_meet = min(near, fall_late) - 1, min(near, rise_late) - 1
    fall_stops, rise_stops = stops(up, fall_late, fall_meet), stops(down, rise_late, rise_meet)

    def part(place, s):
        return partial[place, :, s * part_width : (s + 1) * part_width]

    def fall_copy(k, s):
        return copy_to(
            fall_out.at[k - 1, s], fall_in.at[k - 1, s],
            fall_send.at[k - 1, s], fall_recv.at[k - 1, s], moved(me, n, z=fall_stops[k] - k),
        )

    def rise_copy(k, s):
        return copy_to(
            rise_out.at[k - 1, s], rise_in.at[k - 1, s],
            rise_send.at[k - 1, s], rise_recv.at[k - 1, s], moved(me, n, z=k - rise_stops[k]),
        )

    def settle():
        for d in order:
            if d:
                z_copy(d).wait_send()
            for i in range(len(plane)):
                plane_copy(d, i).wait_send()
            share_copy(d, core).wait_send()
        for c in fold_copies:
            c.wait_send()
        for k in range(up):
            note_up(k).wait_send()
        for k in range(down):
            note_down(k).wait_send()
        for p in range(PIECES):
            for k in range(up):
                up_copy(k, p).wait_send()
            for k in range(down):
                down_copy(k, p).wait_send()
        for q in range(2 * groups):
            core_copy(q, core).wait_send()
            for i in range(len(plane)):
                pick_copy(q, i).wait_send()
        for g in range(groups):
            for i in range(len(plane)):
                ret_copy(g, i).wait_send()
            for i in range(len(tensor_steps)):
                hid_copy(g, i).wait_send()

    def gathered(total, k, s, copy, buffer, where):
        for other in sorted(where):
            if where[other] == k:
                copy(other, s).wait_recv()
                total = total + buffer[other - 1, s].astype(f32)
        return total

    def fall(k):
        for s in range(SPLIT):
            total = gathered(part(2 * k - 1, s), k, s, fall_copy, fall_in, fall_stops)
            fall_out[k - 1, s] = total.astype(bf16)
            fall_copy(k, s).start()

    def rise(k):
        for s in range(SPLIT):
            total = gathered(part(2 * k, s), k, s, rise_copy, rise_in, rise_stops)
            rise_out[k - 1, s] = total.astype(bf16)
            rise_copy(k, s).start()

    def in_turn(*lines):
        for i in range(max(len(ks) for _, ks in lines)):
            for act, ks in lines:
                if i < len(ks):
                    act(ks[i])

    def back_from(high, low):
        return list(range(high, low, -1))

    in_turn(
        (fall, back_from(fall_late - 1, fall_meet)),
        (rise, back_from(rise_late - 1, rise_meet)),
        (fall, back_from(fall_meet - 1, 0)),
        (rise, back_from(rise_meet - 1, 0)),
    )
    mix(groups - 1)
    fall_last = back_from(up, fall_late - 1) + [fall_meet] * (fall_meet > 0)
    rise_last = back_from(down, rise_late - 1) + [rise_meet] * (rise_meet > 0)
    in_turn((fall, fall_last[:1]), (rise, rise_last[:1]))
    settle()
    in_turn((fall, fall_last[1:]), (rise, rise_last[1:]))
    for s in range(SPLIT):
        cols = slice(s * part_width, (s + 1) * part_width)
        total = kept[:, cols].astype(f32) + part(0, s)
        total = gathered(total, 0, s, rise_copy, rise_in, rise_stops)
        mixed_ref[:, cols] = gathered(total, 0, s, fall_copy, fall_in, fall_stops).astype(bf16)

    for s in range(SPLIT):
        for k in range(1, up + 1):
            fall_copy(k, s).wait_send()
        for k in range(1, down + 1):
            rise_copy(k, s).wait_send()


def body(
    q_proj,
    key_projection,
    value_projection,
    segments,
    resid,
    norm_gain,
    route_ids,
    route_gates,
    w_gate,
    w_up,
    w_down,
):
    n = sizes()
    rows, width = q_proj.shape
    plane_rows = n["xh"] * rows
    reach = min(-(-REACH // plane_rows), n["z"] - 1)
    experts = n["xh"] * n["dp"]
    tensors = n["xl"] * n["core"]
    lanes = GROUP * BLOCK
    slabs = tensors * n["dp"]
    up, down = n["z"] // 2, max(n["z"] // 2 - 1, 1)
    groups = n["z"] // GROUP
    half = slabs * width // n["core"]
    out_width = n["dp"] * width
    units = w_gate.shape[1]
    n_slots = experts * SLOTS
    part_width = out_width // SPLIT
    args = (
        q_proj, key_projection, value_projection, segments.reshape(1, -1), resid, norm_gain.reshape(-1, 128),
        route_ids.T, route_gates.T, w_gate, w_up, w_down,
    )
    held = (0, 1, 2, 3, 4, 5, 6, 7, 8, 9, 10)
    buffers = [
        ((2, reach + 1, plane_rows, HEAD_WIDTH), bf16),
        ((rows * width // HEAD_WIDTH, HEAD_WIDTH), bf16),
        ((n["z"], 2, route_ids.shape[1], lanes), f32),
        ((rows, width), bf16),
        ((slabs, BLOCK, width), bf16),
        ((BLOCK, out_width), bf16),
        ((slabs * width // 128, 128), f32),
        ((n["z"], PIECES, BLOCK, half // PIECES), bf16),
        ((2 * groups, experts, SLOTS, half // 2), bf16),
        ((n["core"], 2 * groups, experts, SLOTS, half // 2), bf16),
        ((groups, tensors, units, n_slots), bf16),
        ((groups, experts, SLOTS, out_width), bf16),
        ((groups, experts, SLOTS, out_width), bf16),
        ((n["z"], BLOCK, out_width), f32),
        ((up, SPLIT, BLOCK, part_width), bf16),
        ((up, SPLIT, BLOCK, part_width), bf16),
        ((down, SPLIT, BLOCK, part_width), bf16),
        ((down, SPLIT, BLOCK, part_width), bf16),
    ]
    semaphores = [
        (reach + 1,), (reach + 1, experts), (reach + 1,), (up,), (down,), (slabs,),
        (up, PIECES), (down, PIECES), (2 * groups, experts), (2 * groups,), (groups, tensors), (groups, experts),
        (up, SPLIT), (down, SPLIT),
    ]
    dma = pltpu.SemaphoreType.DMA
    return pl.pallas_call(
        functools.partial(layer_kernel, n),
        out_shape=jax.ShapeDtypeStruct((BLOCK, out_width), bf16),
        in_specs=[pl.BlockSpec(memory_space=pl.ANY)] * len(args),
        out_specs=pl.BlockSpec(memory_space=pltpu.VMEM),
        scratch_shapes=[pltpu.VMEM(args[i].shape, args[i].dtype) for i in held]
        + [pltpu.VMEM(*b) for b in buffers]
        + [dma((len(args),))]
        + [dma(shape) for shape in semaphores for _ in range(2)],
        compiler_params=pltpu.CompilerParams(
            collective_id=0, has_side_effects=True, vmem_limit_bytes=56 * 1024 * 1024
        ),
        name="layer",
    )(*args)


def solution(mesh):
    n_cp, n_tp, n_dp = (mesh.shape[a] for a in ("cp", "tp", "dp"))
    fine = Mesh(
        mesh.devices.reshape(n_cp // 2, 2, n_tp // 2, 2, n_dp), ("z", "xh", "xl", "core", "dp")
    )
    cp, tp = ("z", "xh"), ("xl", "core")
    placed = (
        P(cp, tp + ("dp",)),
        P(cp, None),
        P(cp, None),
        P(),
        P(cp, tp + ("dp",)),
        P(),
        P(cp + ("dp",), None),
        P(cp + ("dp",), None),
        P(cp + ("dp",), tp, None),
        P(cp + ("dp",), tp, None),
        P(cp + ("dp",), None, tp),
    )
    return jax.shard_map(
        body, mesh=fine, in_specs=placed, out_specs=P(cp + ("dp",), tp), check_vma=False
    )
```
